512 devices in a mesh: blk: 16 (over y_hi, x, core), dp: 32 (over y_lo, z).
Axes of the slice: x: 4, y: 4 (y_hi: 2, y_lo: 2; y = y_hi * 2 + y_lo), z: 16, core: 2. Of those that a mesh axis runs over, the one named last changes fastest.
Arguments:
- queries: bfloat16 [32, 1024, 3584], P('dp', 'blk'), may hold values from -0.33407655 to 0.33407655
- passages: bfloat16 [32, 1024, 3584], P('dp', 'blk'), may hold values from -0.10022297 to 0.10022297
- positive: int32 [32, 1024], P('dp'), may hold values from 0 to 1023, as said below
- hard_owner: int32 [32, 1024, 1], P('dp', 'blk'), may hold values from 0 to 31, as said below
- hard_slot: int32 [32, 1024, 1], P('dp', 'blk'), may hold values from 0 to 63
Outputs:
- losses: float32 [32, 1024], P('dp', 'blk')
- question_derivative: bfloat16 [32, 1024, 3584], P('dp', 'blk')
- passage_grad: bfloat16 [32, 1024, 3584], P('dp', 'blk')
The draws below stay inside these ranges and needn't reach their ends.
Inputs may be any that keep to these rules, and one draw needn't show every extreme that they name: `positive`: in each group the entries are a permutation of 0 to 1023. `hard_owner`: the rows of one device name each group at most 3 times, and one group exactly 3 times.
All inputs are finite; a program needn't handle non-finite values.
Results may differ from the reference program's by a relative error of at most 0.006.
Values may be sent and summed in bfloat16 or wider, within the bound.
A program may use at most 128 MiB of HBM per device.

```python
import jax
import jax.numpy as jnp
from jax import lax

D = 3584
ROWS_DEV = 64
HARD = 1
GROUP = 1024
CAPACITY = 3
N_BLK = 16
N_DP = 32


def draw_routing(key):
    base_key = jax.random.fold_in(key, 7)
    key_star, key_rank, key_shuffle, key_slot, key_positive = jax.random.split(base_key, 5)
    block_count = N_DP * N_BLK
    pool_size = N_DP * CAPACITY
    wanted = ROWS_DEV * HARD
    star_owner = jax.random.randint(key_star, (block_count, 1), 0, N_DP)
    entry_owner = jnp.broadcast_to((jnp.arange(pool_size, dtype=jnp.int32) // CAPACITY)[None, :], (block_count, pool_size))
    ranking = jax.random.randint(key_rank, (block_count, pool_size), 0, 2 ** 16) * pool_size + jnp.arange(pool_size, dtype=jnp.int32)[None, :]
    ranking = jnp.where(entry_owner == star_owner, ranking - 2 ** 30, ranking)
    ordering = jnp.argsort(ranking, axis=1, stable=True)
    chosen = jnp.take_along_axis(entry_owner, ordering[:, :wanted], 1)
    shuffle = jax.random.randint(key_shuffle, (block_count, wanted), 0, 2 ** 16) * wanted + jnp.arange(wanted, dtype=jnp.int32)[None, :]
    shuffle = jnp.argsort(shuffle, axis=1, stable=True)
    owner_index = jnp.take_along_axis(chosen, shuffle, 1).reshape(N_DP, GROUP, HARD).astype(jnp.int32)
    slot_rows = jax.random.randint(key_slot, (N_DP, GROUP, HARD), 0, ROWS_DEV).astype(jnp.int32)
    positive_rank = jax.random.randint(key_positive, (N_DP, GROUP), 0, 2 ** 16) * GROUP + jnp.arange(GROUP, dtype=jnp.int32)[None, :]
    correct_target_slot = jnp.argsort(positive_rank, axis=1, stable=True).astype(jnp.int32)
    return (owner_index, slot_rows, correct_target_slot)


def draw_embeddings(key):
    owner_index, slot_rows, correct_target_slot = draw_routing(key)
    base_key = jax.random.fold_in(key, 13)
    key_query, key_passage, key_first, key_second = jax.random.split(base_key, 4)
    full_shape = (N_DP, GROUP, D)
    spread = D ** (-0.5)
    document_embedding_table = jnp.clip(jax.random.normal(key_passage, full_shape, jnp.float32), -6.0, 6.0) * spread
    jitter = jnp.clip(jax.random.normal(key_query, full_shape, jnp.float32), -6.0, 6.0) * spread
    weight_pos = jax.random.uniform(key_first, (N_DP, GROUP, 1), jnp.float32, 0.06, 0.14)
    weight_hard = jax.random.uniform(key_second, (N_DP, GROUP, 1), jnp.float32, 0.04, 0.12)
    row_index = (jnp.arange(GROUP, dtype=jnp.int32) // ROWS_DEV * ROWS_DEV)[None, :, None] + slot_rows
    hard_sum = jnp.sum(document_embedding_table[owner_index, row_index], axis=2)
    positive_rows = jnp.take_along_axis(document_embedding_table, correct_target_slot[:, :, None], axis=1)
    question_embedding_table = weight_pos * positive_rows + weight_hard * hard_sum + jitter
    return (question_embedding_table, document_embedding_table)


def draw_queries(key, part):
    return draw_embeddings(key)[0].astype(jnp.bfloat16)


def draw_passages(key, part):
    return draw_embeddings(key)[1].astype(jnp.bfloat16)


def draw_positive(key, part):
    return draw_routing(key)[2]


def draw_hard_owner(key, part):
    return draw_routing(key)[0]


def draw_hard_slot(key, part):
    return draw_routing(key)[1]


def setup_inputs(seed: int = 0) -> dict:
    splits = jax.random.split(jax.random.key(seed), 6)
    return {
        "queries": draw_queries(jax.random.fold_in(splits[5], 71), 0),
        "passages": draw_passages(jax.random.fold_in(splits[5], 71), 0),
        "positive": draw_positive(jax.random.fold_in(splits[5], 71), 0),
        "hard_owner": draw_hard_owner(jax.random.fold_in(splits[5], 71), 0),
        "hard_slot": draw_hard_slot(jax.random.fold_in(splits[5], 71), 0),
    }


logit_scale_factor = 50.0


def reference(queries, passages, positive, hard_owner, hard_slot):
    block_start = (jnp.arange(GROUP, dtype=jnp.int32) // ROWS_DEV) * ROWS_DEV
    every_row = jnp.arange(GROUP, dtype=jnp.int32)

    def one_group(hard_accum, group_index):
        question_embedding_table = queries[group_index]
        document_embedding_table = passages[group_index]
        correct_target_slot = positive[group_index]
        owner_index = hard_owner[group_index]
        row_index = block_start[:, None] + hard_slot[group_index]
        distractor_documents = passages[owner_index, row_index]
        cosine_logit_table = logit_scale_factor * jnp.dot(question_embedding_table, document_embedding_table.T, preferred_element_type=jnp.float32)
        fetched_distractor_logits = logit_scale_factor * jnp.einsum("ib,ipb->ip", question_embedding_table.astype(jnp.float32), distractor_documents.astype(jnp.float32), precision=lax.Precision.HIGHEST)
        peak = jnp.maximum(jnp.max(cosine_logit_table, 1), jnp.max(fetched_distractor_logits, 1))
        aggregate_objective = jnp.sum(jnp.exp(cosine_logit_table - peak[:, None]), 1) + jnp.sum(jnp.exp(fetched_distractor_logits - peak[:, None]), 1)
        lse = peak + jnp.log(aggregate_objective)
        losses = lse - cosine_logit_table[every_row, correct_target_slot]
        weights = jnp.exp(cosine_logit_table - lse[:, None])
        distractor_attention_shares = jnp.exp(fetched_distractor_logits - lse[:, None])
        pairwise_dot_values = jnp.dot(weights, document_embedding_table.astype(jnp.float32), precision=lax.Precision.HIGHEST)
        pairwise_dot_values = pairwise_dot_values + jnp.einsum("gh,ghd->gd", distractor_attention_shares, distractor_documents.astype(jnp.float32), precision=lax.Precision.HIGHEST)
        question_derivative = logit_scale_factor * pairwise_dot_values - logit_scale_factor * document_embedding_table[correct_target_slot].astype(jnp.float32)
        normalized_exponential_shares = weights.astype(jnp.bfloat16)
        paired_target_logits = jnp.zeros((GROUP, D), jnp.float32).at[correct_target_slot].add(question_embedding_table.astype(jnp.float32))
        within_minibatch_derivative = logit_scale_factor * jnp.dot(normalized_exponential_shares.T, question_embedding_table, preferred_element_type=jnp.float32) - logit_scale_factor * paired_target_logits
        distractor_contributions = (logit_scale_factor * distractor_attention_shares[:, :, None] * question_embedding_table.astype(jnp.float32)[:, None, :]).astype(jnp.bfloat16)
        hard_accum = hard_accum.at[owner_index, row_index].add(distractor_contributions.astype(jnp.float32))
        return hard_accum, (losses, question_derivative.astype(jnp.bfloat16), within_minibatch_derivative)

    start_accum = jnp.zeros((N_DP, GROUP, D), jnp.float32)
    hard_accum, (losses, question_derivative, within_minibatch_derivative) = lax.scan(one_group, start_accum, jnp.arange(N_DP, dtype=jnp.int32))
    passage_grad = (within_minibatch_derivative + hard_accum).astype(jnp.bfloat16)
    return (losses, question_derivative, passage_grad)
```

```python
import functools

import jax
import jax.numpy as jnp
from jax import lax
from jax.experimental import pallas as pl
from jax.experimental.pallas import tpu as pltpu
from jax.sharding import PartitionSpec as P

SCALE = 50.0
MESH = pl.DeviceIdType.MESH
N_X, N_Z, N_DP, CAP = 4, 16, 32, 3
LANES = 128
P_ROWS, Q_ROWS = 96, 80
CHUNK = 512
BF, F32 = jnp.bfloat16, jnp.float32

S_Q, S_P, S_ST, S_DQ, S_DP, S_REQ, S_PF, S_QP, S_HW = 0, 4, 8, 12, 16, 20, 52, 84, 116
N_SEM = 148


def iota(shape, dim):
    return lax.broadcasted_iota(jnp.int32, shape, dim)


def dot(a, b, contract=((1,), (0,))):
    return lax.dot_general(a, b, (contract, ((), ())), preferred_element_type=F32)


def split(a):
    high = a.astype(BF)
    return high, (a - high.astype(F32)).astype(BF)


def kernel(
    meta, q, p, loss_out, qd_out, pg_out,
    qg, pc, pscr, qscr, pbuf, qbuf, precv, qrecv, pn, qn, neg,
    req, req_in, hw, hw_in, stats, stats_in,
    dqf, dqs, dq_in, dpf, dps, dpc_in, dpy, dpy_in,
    send, recv, local,
):
    rows, width = q.shape
    wide = N_X * rows
    chunks = width // CHUNK
    blk, dp = lax.axis_index("blk"), lax.axis_index("dp")
    core, x, yh = lax.rem(blk, 2), lax.rem(blk // 2, N_X), blk // (2 * N_X)
    z, yl = lax.rem(dp, N_Z), dp // N_Z
    other_core, other_yh = blk + 1 - 2 * core, blk + 2 * N_X - 4 * N_X * yh
    mine, across = yh * 2 + core, (1 - yh) * 2 + core

    def x_peer(d):
        to = lax.rem(x + d, N_X)
        return to, (yh * N_X + to) * 2 + core

    def dp_peer(t):
        dy = lax.rem(t, 2)
        k = t // 2
        half = (k + 1) // 2
        odd = lax.rem(k, 2)
        dz = lax.rem(N_Z // 2 + half - 2 * half * odd + N_Z, N_Z)
        return (
            lax.rem(yl + dy, 2) * N_Z + lax.rem(z + dz, N_Z),
            lax.rem(yl + dy, 2) * N_Z + lax.rem(z - dz + N_Z, N_Z),
        )

    self_t = 2 * (N_Z - 1)

    def each_partner(act):
        def step(t, carry):
            act(t)
            return carry

        lax.fori_loop(0, self_t, step, 0)
        act(self_t + 1)

    def remote(src, dst, slot, **to):
        return pltpu.make_async_remote_copy(
            src_ref=src,
            dst_ref=dst,
            send_sem=send.at[slot],
            recv_sem=recv.at[slot],
            device_id={"blk": blk, "dp": dp, **to},
            device_id_type=MESH,
        )

    barrier = pltpu.get_barrier_semaphore()

    def greet(**to):
        pl.semaphore_signal(barrier, inc=1, device_id={"blk": blk, "dp": dp, **to}, device_id_type=MESH)

    for d in range(1, N_X):
        greet(blk=x_peer(d)[1])
    greet(blk=other_core)
    greet(blk=other_yh)
    each_partner(lambda t: greet(dp=dp_peer(t)[0]))

    keep_q = pltpu.make_async_copy(q, qg.at[x], local.at[0])
    keep_p = pltpu.make_async_copy(p, pc.at[mine], local.at[1])
    keep_q.start()
    keep_p.start()

    owner_row = meta[1:2, :rows].astype(F32)
    slot_row = meta[2:3, :rows].astype(F32)
    r0, r1 = iota((rows, rows), 0), iota((rows, rows), 1)
    eye = r0 == r1

    def column(row):
        return jnp.sum(jnp.where(eye, row, 0.0), axis=1, keepdims=True)

    owner_col = column(owner_row)
    same = jnp.where(owner_col == owner_row, 1.0, 0.0)
    rank_col = jnp.sum(jnp.where(r1 < r0, same, 0.0), axis=1, keepdims=True)
    rank_row = jnp.sum(jnp.where(r0 < r1, same, 0.0), axis=0, keepdims=True)
    key_row = rank_row * N_DP + owner_row
    key_col = rank_col * N_DP + owner_col
    slots = N_DP * CAP
    by_slot = key_row == iota((slots, rows), 0).astype(F32)
    by_row = key_col == iota((rows, slots), 1).astype(F32)
    lane = iota((N_DP, LANES), 1)

    def table(row):
        out = jnp.zeros((N_DP, LANES), F32)
        for c in range(CAP):
            picked = jnp.where(by_slot[c * N_DP : (c + 1) * N_DP], row, 0.0)
            out = jnp.where(lane == c, jnp.sum(picked, axis=1, keepdims=True), out)
        return out

    every_8th = pl.ds(0, N_DP, stride=8)
    stats[...] = jnp.zeros_like(stats)
    req[...] = jnp.zeros_like(req)
    hw[...] = jnp.zeros_like(hw)
    req[every_8th, :] = table(slot_row + 1.0)
    pscr[...] = jnp.zeros_like(pscr)

    pl.semaphore_wait(barrier, N_X + 1 + N_DP - 1)

    def table_copy(src, dst, base, t):
        to, _ = dp_peer(t)
        return remote(
            src.at[pl.ds(pl.multiple_of(to * 8, 8), 8)],
            dst.at[pl.ds(pl.multiple_of(dp * 8, 8), 8)],
            base + t,
            dp=to,
        )

    def rows_copy(src, dst, base, t):
        to, _ = dp_peer(t)
        return remote(src.at[to], dst.at[dp], base + t, dp=to)

    request = functools.partial(table_copy, req, req_in, S_REQ)
    weight = functools.partial(table_copy, hw, hw_in, S_HW)
    fetch = functools.partial(rows_copy, pbuf, precv, S_PF)
    push = functools.partial(rows_copy, qbuf, qrecv, S_QP)

    each_partner(lambda t: request(t).start())

    q_copies = [remote(q, qg.at[x], S_Q + d, blk=x_peer(d)[1]) for d in range(1, N_X)]
    p_core = remote(p, pc.at[mine], S_P, blk=other_core)
    p_across = remote(p, pc.at[mine], S_P + 1, blk=other_yh)
    p_across.start()
    for copy in q_copies:
        copy.start()
    p_core.start()

    def lay_out(onehot, source, place):
        for n in range(chunks):
            packed = dot(onehot, source[:, n * CHUNK : (n + 1) * CHUNK])
            for c in range(CAP):
                for k in range(CHUNK // LANES):
                    ref, at, stride = place(c * (width // LANES) + n * (CHUNK // LANES) + k)
                    ref[pl.ds(at, N_DP, stride=stride), :] = packed[
                        c * N_DP : (c + 1) * N_DP, k * LANES : (k + 1) * LANES
                    ]

    def place_q(i):
        return (qscr, i, Q_ROWS) if i < Q_ROWS else (pscr, 84 + i - Q_ROWS, P_ROWS)

    def place_p(i):
        return (pscr, i, P_ROWS)

    lay_out(jnp.where(by_slot, 1.0, 0.0).astype(BF), q, place_q)

    def round_q(a, carry):
        qbuf[a] = qscr[pl.ds(pl.multiple_of(a * Q_ROWS, 16), Q_ROWS), :].astype(BF)
        return carry

    lax.fori_loop(0, N_DP, round_q, 0)

    each_partner(lambda t: request(t).wait_recv())
    req_in[pl.ds(pl.multiple_of(dp * 8, 8), 8), :] = req[pl.ds(pl.multiple_of(dp * 8, 8), 8), :]
    asked = req_in[every_8th, :] - 1.0

    def by_asked(values):
        row_of = iota((N_DP, rows), 1).astype(F32)
        return jnp.concatenate(
            [jnp.where(asked[:, c : c + 1] == row_of, values[:, c : c + 1], 0.0) for c in range(CAP)],
            axis=0,
        )

    lay_out(by_asked(jnp.ones((N_DP, LANES), F32)).astype(BF), p, place_p)

    def round_p(a, carry):
        pbuf[a] = pscr[pl.ds(pl.multiple_of(a * P_ROWS, 16), P_ROWS), :].astype(BF)
        return carry

    lax.fori_loop(0, N_DP, round_p, 0)
    each_partner(lambda t: fetch(t).start())
    each_partner(lambda t: push(t).start())
    precv[dp] = pbuf[dp]
    qrecv[dp] = qbuf[dp]

    p_across.wait_recv()
    p_pass = remote(pc.at[across], pc.at[across], S_P + 2, blk=other_core)
    p_pass.start()
    keep_q.wait()
    keep_p.wait()
    for copy in q_copies:
        copy.wait_recv()
    p_core.wait_recv()
    p_pass.wait_recv()

    def columns(n):
        return pl.ds(pl.multiple_of(n * CHUNK, CHUNK), CHUNK)

    def add_scores(n, total):
        return total + dot(
            pc[:, :, columns(n)].reshape(wide, CHUNK),
            qg[:, :, columns(n)].reshape(wide, CHUNK),
            ((1,), (1,)),
        )

    scores = SCALE * lax.fori_loop(0, chunks, add_scores, jnp.zeros((wide, wide), F32))
    row = iota((wide, 1), 0)
    index = ((row // (2 * rows)) * N_X + x) * 2 * rows + lax.rem(row, 2 * rows)
    paired = jnp.where(index == meta[0:1, :], 1.0, 0.0)
    peak = jnp.max(scores, axis=0, keepdims=True)
    total = jnp.sum(jnp.exp(scores - peak), axis=0, keepdims=True)
    picked = jnp.sum(paired * scores, axis=0, keepdims=True)

    each_partner(lambda t: fetch(t).wait_recv())

    def widen_p(a, carry):
        pscr[pl.ds(pl.multiple_of(a * P_ROWS, 8), P_ROWS), :] = precv[a].astype(F32)
        return carry

    lax.fori_loop(0, N_DP, widen_p, 0)

    def gather_rows(out, place):
        for n in range(width // LANES):
            for c in range(CAP):
                ref, at, stride = place(c * (width // LANES) + n)
                out[c * N_DP : (c + 1) * N_DP, n * LANES : (n + 1) * LANES] = ref[
                    pl.ds(at, N_DP, stride=stride), :
                ].astype(BF)

    gather_rows(pn, place_p)
    pick = jnp.where(by_row, 1.0, 0.0).astype(BF)

    def take_negatives(n, total):
        rows_of = dot(pick, pn[:, columns(n)])
        neg[:, columns(n)] = rows_of.astype(BF)
        return total + rows_of * q[:, columns(n)].astype(F32)

    products = lax.fori_loop(0, chunks, take_negatives, jnp.zeros((rows, CHUNK), F32))
    hard_col = SCALE * jnp.sum(products, axis=1, keepdims=True)
    shifted = iota((rows, wide), 1) == iota((rows, wide), 0) + x * rows
    hard_wide = jnp.sum(jnp.where(shifted, hard_col, 0.0), axis=0, keepdims=True)
    own = iota((1, wide), 1) // rows == x
    peak_own = jnp.where(own, jnp.maximum(peak, hard_wide), peak)
    total = total * jnp.exp(peak - peak_own) + jnp.where(own, jnp.exp(hard_wide - peak_own), 0.0)
    stats[0:1, :] = peak_own
    stats[1:2, :] = total
    stats[2:3, :] = picked
    st_copies = [remote(stats, stats_in.at[x], S_ST + d, blk=x_peer(d)[1]) for d in range(1, N_X)]
    for copy in st_copies:
        copy.start()
    stats_in[x] = stats[...]
    for copy in st_copies:
        copy.wait_recv()
    peaks = [stats_in[i, 0:1, :] for i in range(N_X)]
    top = functools.reduce(jnp.maximum, peaks)
    whole = sum(stats_in[i, 1:2, :] * jnp.exp(peaks[i] - top) for i in range(N_X))
    lse = top + jnp.log(whole)
    loss_wide = lse - sum(stats_in[i, 2:3, :] for i in range(N_X))

    def own_column(wide_row):
        return jnp.sum(jnp.where(shifted, wide_row, 0.0), axis=1, keepdims=True)

    loss_out[...] = jnp.sum(jnp.where(eye, own_column(loss_wide), 0.0), axis=0, keepdims=True)
    hard_weight_col = jnp.exp(hard_col - own_column(lse))
    hard_weight_row = jnp.sum(jnp.where(eye, hard_weight_col, 0.0), axis=0, keepdims=True)
    hw[every_8th, :] = table(hard_weight_row)
    each_partner(lambda t: weight(t).start())

    weights = jnp.exp(scores - lse)
    high, low = split((weights - paired).T)

    def query_terms(n, carry):
        part = pc[:, :, columns(n)].reshape(wide, CHUNK)
        out = (SCALE * (dot(high, part) + dot(low, part))).reshape(N_X, rows, CHUNK)
        dqf[:, :, columns(n)] = out
        dqs[:, :, columns(n)] = out.astype(BF)
        return carry

    lax.fori_loop(0, chunks, query_terms, 0)
    dq_copies = [
        remote(dqs.at[x_peer(d)[0]], dq_in.at[d], S_DQ + d, blk=x_peer(d)[1]) for d in range(1, N_X)
    ]
    for copy in dq_copies:
        copy.start()

    probs, pairs = weights.astype(BF), paired.astype(BF)

    def passage_terms(n, carry):
        part = qg[:, :, columns(n)].reshape(wide, CHUNK)
        out = (SCALE * (dot(probs, part) - dot(pairs, part))).reshape(N_X, rows, CHUNK)
        dpf[:, :, columns(n)] = out
        dps[:, :, columns(n)] = out.astype(BF)
        return carry

    lax.fori_loop(0, chunks, passage_terms, 0)
    dp_across = remote(dps.at[(1 - yh) * 2 + 1 - core], dpc_in.at[1], S_DP, blk=other_core)
    dp_here = remote(dps.at[yh * 2 + 1 - core], dpc_in.at[0], S_DP + 1, blk=other_core)
    dp_across.start()
    dp_here.start()
    dp_across.wait_recv()

    def sum_across(n, carry):
        dpy[:, columns(n)] = (dpf[across, :, columns(n)] + dpc_in[1, :, columns(n)].astype(F32)).astype(BF)
        return carry

    lax.fori_loop(0, chunks, sum_across, 0)
    dp_y = remote(dpy, dpy_in, S_DP + 2, blk=other_yh)
    dp_y.start()

    for copy in dq_copies:
        copy.wait_recv()

    def query_sum(n, carry):
        out = dqf[x, :, columns(n)] + SCALE * hard_weight_col * neg[:, columns(n)].astype(F32)
        for d in range(1, N_X):
            out = out + dq_in[d, :, columns(n)].astype(F32)
        qd_out[:, columns(n)] = out.astype(BF)
        return carry

    lax.fori_loop(0, chunks, query_sum, 0)

    each_partner(lambda t: weight(t).wait_recv())
    hw_in[pl.ds(pl.multiple_of(dp * 8, 8), 8), :] = hw[pl.ds(pl.multiple_of(dp * 8, 8), 8), :]
    hard_high, hard_low = split(by_asked(hw_in[every_8th, :]).T)
    each_partner(lambda t: push(t).wait_recv())

    def widen_q(a, carry):
        qscr[pl.ds(pl.multiple_of(a * Q_ROWS, 8), Q_ROWS), :] = qrecv[a].astype(F32)
        return carry

    lax.fori_loop(0, N_DP, widen_q, 0)
    gather_rows(qn, place_q)
    dp_here.wait_recv()
    dp_y.wait_recv()

    def passage_sum(n, carry):
        terms = qn[:, columns(n)]
        out = dpf[mine, :, columns(n)] + SCALE * (dot(hard_high, terms) + dot(hard_low, terms))
        out = out + dpc_in[0, :, columns(n)].astype(F32) + dpy_in[:, columns(n)].astype(F32)
        pg_out[:, columns(n)] = out.astype(BF)
        return carry

    lax.fori_loop(0, chunks, passage_sum, 0)

    for copy in (*q_copies, p_core, p_across, p_pass, *st_copies, *dq_copies, dp_across, dp_here, dp_y):
        copy.wait_send()

    def sent(t):
        request(t).wait_send()
        fetch(t).wait_send()
        push(t).wait_send()
        weight(t).wait_send()

    each_partner(sent)


def shards(queries, passages, positive, hard_owner, hard_slot):
    q, p = queries[0], passages[0]
    rows, width = q.shape
    wide = N_X * rows
    blk = lax.axis_index("blk")
    places = positive.reshape(2, N_X, 2, rows)
    places = lax.dynamic_index_in_dim(places, blk // (2 * N_X), 0, keepdims=False)
    places = lax.dynamic_index_in_dim(places, lax.rem(blk, 2), 1, keepdims=False)
    pad = ((0, 0), (0, wide - rows))
    meta = jnp.concatenate(
        [
            places.reshape(1, wide),
            jnp.pad(hard_owner.reshape(1, rows), pad),
            jnp.pad(hard_slot.reshape(1, rows), pad),
        ],
        axis=0,
    )
    vmem = pl.BlockSpec(memory_space=pltpu.VMEM)
    block = (rows, width)
    loss, qd, pg = pl.pallas_call(
        kernel,
        out_shape=(
            jax.ShapeDtypeStruct((1, rows), F32),
            jax.ShapeDtypeStruct(block, BF),
            jax.ShapeDtypeStruct(block, BF),
        ),
        in_specs=[vmem] * 3,
        out_specs=[vmem] * 3,
        scratch_shapes=[
            pltpu.VMEM((N_X, *block), BF),
            pltpu.VMEM((N_X, *block), BF),
            pltpu.VMEM((N_DP * P_ROWS, LANES), F32),
            pltpu.VMEM((N_DP * Q_ROWS, LANES), F32),
            pltpu.VMEM((N_DP, P_ROWS, LANES), BF),
            pltpu.VMEM((N_DP, Q_ROWS, LANES), BF),
            pltpu.VMEM((N_DP, P_ROWS, LANES), BF),
            pltpu.VMEM((N_DP, Q_ROWS, LANES), BF),
            pltpu.VMEM((N_DP * CAP, width), BF),
            pltpu.VMEM((N_DP * CAP, width), BF),
            pltpu.VMEM(block, BF),
            pltpu.VMEM((N_DP * 8, LANES), F32),
            pltpu.VMEM((N_DP * 8, LANES), F32),
            pltpu.VMEM((N_DP * 8, LANES), F32),
            pltpu.VMEM((N_DP * 8, LANES), F32),
            pltpu.VMEM((8, wide), F32),
            pltpu.VMEM((N_X, 8, wide), F32),
            pltpu.VMEM((N_X, *block), F32),
            pltpu.VMEM((N_X, *block), BF),
            pltpu.VMEM((N_X, *block), BF),
            pltpu.VMEM((N_X, *block), F32),
            pltpu.VMEM((N_X, *block), BF),
            pltpu.VMEM((2, *block), BF),
            pltpu.VMEM(block, BF),
            pltpu.VMEM(block, BF),
            pltpu.SemaphoreType.DMA((N_SEM,)),
            pltpu.SemaphoreType.DMA((N_SEM,)),
            pltpu.SemaphoreType.DMA((2,)),
        ],
        compiler_params=pltpu.CompilerParams(
            collective_id=0, has_side_effects=True, vmem_limit_bytes=56 * 2**20
        ),
        cost_estimate=pl.CostEstimate(flops=3 * 10**9, bytes_accessed=2 * 10**6, transcendentals=2 * 10**5),
    )(meta, q, p)
    return loss, qd[None], pg[None]


def solution(mesh):
    placed = (
        P("dp", "blk", None),
        P("dp", "blk", None),
        P("dp", None),
        P("dp", "blk", None),
        P("dp", "blk", None),
    )
    return jax.shard_map(
        shards,
        mesh=mesh,
        in_specs=placed,
        out_specs=(P("dp", "blk"), P("dp", "blk", None), P("dp", "blk", None)),
        check_vma=False,
    )
```

```python
import functools

import jax
import jax.numpy as jnp
from jax import lax
from jax.experimental import pallas as pl
from jax.experimental.pallas import tpu as pltpu
from jax.sharding import PartitionSpec as P

SCALE = 50.0
MESH = pl.DeviceIdType.MESH
N_X, N_Z, N_DP, CAP = 4, 16, 32, 3
LANES = 128
P_ROWS, Q_ROWS = 96, 80
CHUNK = 512
BF, F32 = jnp.bfloat16, jnp.float32

S_Q, S_P, S_ST, S_DP, S_AL, S_DQ, S_PP, S_REQ, S_PF, S_QP, S_HW = 0, 4, 8, 12, 16, 20, 26, 32, 64, 96, 128
N_SEM = 160
EARLY = 4


def iota(shape, dim):
    return lax.broadcasted_iota(jnp.int32, shape, dim)


def dot(a, b, contract=((1,), (0,))):
    return lax.dot_general(a, b, (contract, ((), ())), preferred_element_type=F32)


def split(a):
    high = a.astype(BF)
    return high, (a - high.astype(F32)).astype(BF)


def kernel(
    positive, owner, slot, q_in, p_in, loss_out, qd_out, pg_out,
    qg, pc, pscr, qscr, pbuf, qbuf, precv, qrecv, pn, qn, neg,
    req, req_in, hw, hw_in, stats, stats_in, alphas, alphas_in,
    tf, ts, t_in, t_pass, t_sum, pps, pp_in, pp_pass, pp_sum, dpf, dps, dpc_in, dpy, dpy_in,
    send, recv, local,
):
    rows, width = q_in.shape
    wide = N_X * rows
    chunks = width // CHUNK
    blk, dp = lax.axis_index("blk"), lax.axis_index("dp")
    core, x, yh = lax.rem(blk, 2), lax.rem(blk // 2, N_X), blk // (2 * N_X)
    z, yl = lax.rem(dp, N_Z), dp // N_Z
    other_core, other_yh = blk + 1 - 2 * core, blk + 2 * N_X - 4 * N_X * yh
    mine, across = yh * 2 + core, (1 - yh) * 2 + core

    def x_peer(d):
        to = lax.rem(x + d, N_X)
        return to, (yh * N_X + to) * 2 + core

    right_x, right = x_peer(1)
    left_x, left = x_peer(N_X - 1)
    opposite = lax.rem(x + 2, N_X)
    half = width // 2
    low_half, high_half = pl.ds(0, half), pl.ds(half, half)

    def dp_peer(t):
        dy = lax.rem(t, 2)
        k = t // 2
        half = (k + 1) // 2
        odd = lax.rem(k, 2)
        dz = lax.rem(N_Z // 2 + half - 2 * half * odd + N_Z, N_Z)
        y = lax.rem(yl + dy, 2) * N_Z
        return y + lax.rem(z + dz, N_Z), y + lax.rem(z - dz + N_Z, N_Z)

    self_t = 2 * (N_Z - 1)

    def each_partner(act, first=0):
        def step(t, carry):
            act(t)
            return carry

        lax.fori_loop(first, self_t, step, 0)
        act(self_t + 1)

    def remote(src, dst, sem, **to):
        return pltpu.make_async_remote_copy(
            src_ref=src,
            dst_ref=dst,
            send_sem=send.at[sem],
            recv_sem=recv.at[sem],
            device_id={"blk": blk, "dp": dp, **to},
            device_id_type=MESH,
        )

    barrier = pltpu.get_barrier_semaphore()

    def greet(**to):
        pl.semaphore_signal(barrier, inc=1, device_id={"blk": blk, "dp": dp, **to}, device_id_type=MESH)

    each_partner(lambda t: greet(dp=dp_peer(t)[0]))
    for d in range(1, N_X):
        greet(blk=x_peer(d)[1])
    greet(blk=other_core)
    greet(blk=other_yh)

    keep_q = pltpu.make_async_copy(q_in, qg.at[x], local.at[0])
    keep_p = pltpu.make_async_copy(p_in, pc.at[mine], local.at[1])
    keep_q.start()
    keep_p.start()

    owner_row = owner[...].astype(F32)
    slot_row = slot[...].astype(F32)
    r0, r1 = iota((rows, rows), 0), iota((rows, rows), 1)
    eye = r0 == r1

    def column(row):
        return jnp.sum(jnp.where(eye, row, 0.0), axis=1, keepdims=True)

    owner_col = column(owner_row)
    same = jnp.where(owner_col == owner_row, 1.0, 0.0)
    rank_col = jnp.sum(jnp.where(r1 < r0, same, 0.0), axis=1, keepdims=True)
    rank_row = jnp.sum(jnp.where(r0 < r1, same, 0.0), axis=0, keepdims=True)
    key_row = rank_row * N_DP + owner_row
    key_col = rank_col * N_DP + owner_col
    slots = N_DP * CAP
    by_slot = key_row == iota((slots, rows), 0).astype(F32)
    by_row = key_col == iota((rows, slots), 1).astype(F32)
    lane = iota((N_DP, LANES), 1)

    def table(row):
        out = jnp.zeros((N_DP, LANES), F32)
        for c in range(CAP):
            picked = jnp.where(by_slot[c * N_DP : (c + 1) * N_DP], row, 0.0)
            out = jnp.where(lane == c, jnp.sum(picked, axis=1, keepdims=True), out)
        return out

    every_8th = pl.ds(0, N_DP, stride=8)
    req[...] = jnp.zeros_like(req)
    req[every_8th, :] = table(slot_row + 1.0)
    hw[...] = jnp.zeros_like(hw)
    stats[...] = jnp.zeros_like(stats)
    alphas[...] = jnp.zeros_like(alphas)
    pscr[...] = jnp.zeros_like(pscr)

    def columns(n):
        return pl.ds(pl.multiple_of(n * CHUNK, CHUNK), CHUNK)

    def lay_out(onehot, ref_of, place):
        for n in range(chunks):
            packed = dot(onehot, ref_of(n))
            for c in range(CAP):
                for k in range(CHUNK // LANES):
                    ref, at, stride = place(c * (width // LANES) + n * (CHUNK // LANES) + k)
                    ref[pl.ds(at, N_DP, stride=stride), :] = packed[
                        c * N_DP : (c + 1) * N_DP, k * LANES : (k + 1) * LANES
                    ]

    def place_q(i):
        return (qscr, i, Q_ROWS) if i < Q_ROWS else (pscr, 84 + i - Q_ROWS, P_ROWS)

    def place_p(i):
        return (pscr, i, P_ROWS)

    keep_q.wait()
    lay_out(
        jnp.where(by_slot, 1.0, 0.0).astype(BF),
        lambda n: qg[x, :, n * CHUNK : (n + 1) * CHUNK],
        place_q,
    )

    def round_q(a, carry):
        qbuf[a] = qscr[pl.ds(pl.multiple_of(a * Q_ROWS, 16), Q_ROWS), :].astype(BF)
        return carry

    lax.fori_loop(0, N_DP, round_q, 0)
    keep_p.wait()
    pl.semaphore_wait(barrier, N_X + 1 + N_DP - 1)

    def table_copy(src, dst, base, t):
        to, _ = dp_peer(t)
        return remote(
            src.at[pl.ds(pl.multiple_of(to * 8, 8), 8)],
            dst.at[pl.ds(pl.multiple_of(dp * 8, 8), 8)],
            base + t,
            dp=to,
        )

    def rows_copy(src, dst, base, t):
        to, _ = dp_peer(t)
        return remote(src.at[to], dst.at[dp], base + t, dp=to)

    request = functools.partial(table_copy, req, req_in, S_REQ)
    weight = functools.partial(table_copy, hw, hw_in, S_HW)
    fetch = functools.partial(rows_copy, pbuf, precv, S_PF)
    push = functools.partial(rows_copy, qbuf, qrecv, S_QP)

    each_partner(lambda t: request(t).start())
    for t in range(EARLY):
        push(t).start()

    q_right = remote(qg.at[x], qg.at[x], S_Q, blk=right)
    q_left = remote(qg.at[x], qg.at[x], S_Q + 1, blk=left)
    p_core = remote(pc.at[mine], pc.at[mine], S_P, blk=other_core)
    p_across = remote(pc.at[mine], pc.at[mine], S_P + 1, blk=other_yh)
    p_across.start()
    q_right.start()
    q_left.start()
    p_core.start()

    each_partner(lambda t: request(t).wait_recv())
    req_in[pl.ds(pl.multiple_of(dp * 8, 8), 8), :] = req[pl.ds(pl.multiple_of(dp * 8, 8), 8), :]
    asked = req_in[every_8th, :] - 1.0

    def by_asked(values):
        row_of = iota((N_DP, rows), 1).astype(F32)
        return jnp.concatenate(
            [jnp.where(asked[:, c : c + 1] == row_of, values[:, c : c + 1], 0.0) for c in range(CAP)],
            axis=0,
        )

    lay_out(
        by_asked(jnp.ones((N_DP, LANES), F32)).astype(BF),
        lambda n: pc[mine, :, n * CHUNK : (n + 1) * CHUNK],
        place_p,
    )

    def round_p(a, carry):
        pbuf[a] = pscr[pl.ds(pl.multiple_of(a * P_ROWS, 16), P_ROWS), :].astype(BF)
        return carry

    lax.fori_loop(0, N_DP, round_p, 0)
    each_partner(lambda t: fetch(t).start())
    each_partner(lambda t: push(t).start(), EARLY)
    precv[dp] = pbuf[dp]
    qrecv[dp] = qbuf[dp]

    p_across.wait_recv()
    p_pass = remote(pc.at[across], pc.at[across], S_P + 2, blk=other_core)
    p_pass.start()
    q_right.wait_recv()
    q_on = remote(qg.at[left_x, :, low_half], qg.at[left_x, :, low_half], S_Q + 2, blk=right)
    q_on.start()
    q_left.wait_recv()
    q_back = remote(qg.at[right_x, :, high_half], qg.at[right_x, :, high_half], S_Q + 3, blk=left)
    q_back.start()

    lanes = iota((8, LANES), 1)
    halves = []
    for i in range(N_X):
        chunk = positive[0:1, pl.ds(pl.multiple_of((yh * N_X + i) * LANES, LANES), LANES)]
        chunk = jnp.broadcast_to(chunk, (8, LANES))
        halves.append(jnp.where(core == i % 2, chunk, pltpu.roll(chunk, rows, 1)))
    positive_wide = jnp.concatenate(
        [jnp.where(lanes < rows, halves[i], halves[i + 1]) for i in range(0, N_X, 2)], axis=1
    )[0:1, :]
    row = iota((wide, 1), 0)
    index = ((row // (2 * rows)) * N_X + x) * 2 * rows + lax.rem(row, 2 * rows)
    paired = jnp.where(index == positive_wide, 1.0, 0.0)

    p_core.wait_recv()
    p_pass.wait_recv()

    pairs = paired.astype(BF)
    pairs_by_query = paired.T.astype(BF)

    def ring_first(blocks, passing, into, base):
        copies = [
            remote(blocks.at[opposite, :, low_half], passing.at[0], base, blk=right),
            remote(blocks.at[opposite, :, high_half], passing.at[1], base + 1, blk=left),
            remote(blocks.at[right_x, :, high_half], into.at[0, :, high_half], base + 2, blk=right),
            remote(blocks.at[left_x, :, low_half], into.at[1, :, low_half], base + 3, blk=left),
        ]
        for copy in copies:
            copy.start()
        return copies

    def ring_second(copies, blocks, passing, sums, into, base):
        copies[0].wait_recv()
        copies[1].wait_recv()
        size = half // chunks

        def add(n, carry):
            at = pl.ds(pl.multiple_of(n * size, size), size)
            beyond = pl.ds(pl.multiple_of(half + n * size, size), size)
            sums[0, :, at] = (blocks[right_x, :, at].astype(F32) + passing[0, :, at].astype(F32)).astype(BF)
            sums[1, :, at] = (blocks[left_x, :, beyond].astype(F32) + passing[1, :, at].astype(F32)).astype(BF)
            return carry

        lax.fori_loop(0, chunks, add, 0)
        more = [
            remote(sums.at[0], into.at[0, :, low_half], base + 4, blk=right),
            remote(sums.at[1], into.at[1, :, high_half], base + 5, blk=left),
        ]
        for copy in more:
            copy.start()
        return copies + more

    q_on.wait_recv()
    q_back.wait_recv()

    def add_scores(n, total):
        return total + dot(
            pc[:, :, columns(n)].reshape(wide, CHUNK),
            qg[:, :, columns(n)].reshape(wide, CHUNK),
            ((1,), (1,)),
        )

    scores = SCALE * lax.fori_loop(0, chunks, add_scores, jnp.zeros((wide, wide), F32))
    peak = jnp.max(scores, axis=0, keepdims=True)
    stats[0:1, :] = peak
    stats[1:2, :] = jnp.sum(jnp.exp(scores - peak), axis=0, keepdims=True)
    stats[2:3, :] = jnp.sum(paired * scores, axis=0, keepdims=True)
    st_copies = [remote(stats, stats_in.at[x], S_ST + d, blk=x_peer(d)[1]) for d in range(1, N_X)]
    for copy in st_copies:
        copy.start()
    stats_in[x] = stats[...]
    for copy in st_copies:
        copy.wait_recv()
    peaks = [stats_in[i, 0:1, :] for i in range(N_X)]
    top = functools.reduce(jnp.maximum, peaks)
    whole = sum(stats_in[i, 1:2, :] * jnp.exp(peaks[i] - top) for i in range(N_X))
    lse_batch = top + jnp.log(whole)
    picked = sum(stats_in[i, 2:3, :] for i in range(N_X))
    weights = jnp.exp(scores - lse_batch)
    high, low = split((weights - paired).T)

    def query_terms(n, carry):
        part = pc[:, :, columns(n)].reshape(wide, CHUNK)
        out = (dot(high, part) + dot(low, part)).reshape(N_X, rows, CHUNK)
        tf[:, :, columns(n)] = out
        ts[:, :, columns(n)] = out.astype(BF)
        return carry

    lax.fori_loop(0, chunks, query_terms, 0)
    t_copies = ring_first(ts, t_pass, t_in, S_DQ)
    def positives(n, carry):
        out = dot(pairs_by_query, pc[:, :, columns(n)].reshape(wide, CHUNK))
        pps[:, :, columns(n)] = out.reshape(N_X, rows, CHUNK).astype(BF)
        return carry

    lax.fori_loop(0, chunks, positives, 0)

    t_copies = ring_second(t_copies, tf, t_pass, t_sum, t_in, S_DQ)

    def widen_p(t):
        fetch(t).wait_recv()
        widen(pscr, precv, P_ROWS, dp_peer(t)[1])

    def widen(out, source, size, a):
        out[pl.ds(pl.multiple_of(a * size, 8), size), :] = source[a].astype(F32)

    widen(pscr, precv, P_ROWS, dp)
    each_partner(widen_p)

    def gather_rows(out, place):
        for n in range(width // LANES):
            for c in range(CAP):
                ref, at, stride = place(c * (width // LANES) + n)
                out[c * N_DP : (c + 1) * N_DP, n * LANES : (n + 1) * LANES] = ref[
                    pl.ds(at, N_DP, stride=stride), :
                ].astype(BF)

    gather_rows(pn, place_p)
    pick = jnp.where(by_row, 1.0, 0.0).astype(BF)

    def take_negatives(n, total):
        rows_of = dot(pick, pn[:, columns(n)])
        neg[:, columns(n)] = rows_of.astype(BF)
        return total + rows_of * qg[x, :, columns(n)].astype(F32)

    products = lax.fori_loop(0, chunks, take_negatives, jnp.zeros((rows, CHUNK), F32))
    hard_col = SCALE * jnp.sum(products, axis=1, keepdims=True)
    shifted = iota((rows, wide), 1) == iota((rows, wide), 0) + x * rows

    def own_column(wide_row):
        return jnp.sum(jnp.where(shifted, wide_row, 0.0), axis=1, keepdims=True)

    batch_col = own_column(lse_batch)
    top_col = jnp.maximum(batch_col, hard_col)
    lse_col = top_col + jnp.log(jnp.exp(batch_col - top_col) + jnp.exp(hard_col - top_col))
    alpha_col = jnp.exp(batch_col - lse_col)
    hard_weight_col = jnp.exp(hard_col - lse_col)
    alphas[0:1, :] = jnp.sum(jnp.where(shifted, alpha_col, 0.0), axis=0, keepdims=True)
    al_copies = [remote(alphas, alphas_in.at[x], S_AL + d, blk=x_peer(d)[1]) for d in range(1, N_X)]
    for copy in al_copies:
        copy.start()
    pp_copies = ring_first(pps, pp_pass, pp_in, S_PP)
    alphas_in[x] = alphas[...]
    hard_weight_row = jnp.sum(jnp.where(eye, hard_weight_col, 0.0), axis=0, keepdims=True)
    hw[every_8th, :] = table(hard_weight_row)
    each_partner(lambda t: weight(t).start())
    for copy in al_copies:
        copy.wait_recv()
    alpha = sum(alphas_in[i, 0:1, :] for i in range(N_X))
    probs = (weights * alpha).astype(BF)

    def passage_terms(n, carry):
        part = qg[:, :, columns(n)].reshape(wide, CHUNK)
        out = (SCALE * (dot(probs, part) - dot(pairs, part))).reshape(N_X, rows, CHUNK)
        dpf[:, :, columns(n)] = out
        dps[:, :, columns(n)] = out.astype(BF)
        return carry

    lax.fori_loop(0, chunks, passage_terms, 0)
    dp_across = remote(dps.at[(1 - yh) * 2 + 1 - core], dpc_in.at[1], S_DP, blk=other_core)
    dp_here = remote(dps.at[yh * 2 + 1 - core], dpc_in.at[0], S_DP + 1, blk=other_core)
    dp_across.start()
    dp_here.start()
    dp_across.wait_recv()

    def sum_across(n, carry):
        dpy[:, columns(n)] = (dpf[across, :, columns(n)] + dpc_in[1, :, columns(n)].astype(F32)).astype(BF)
        return carry

    lax.fori_loop(0, chunks, sum_across, 0)
    dp_y = remote(dpy, dpy_in, S_DP + 2, blk=other_yh)
    dp_y.start()
    pp_copies = ring_second(pp_copies, pps, pp_pass, pp_sum, pp_in, S_PP)

    loss_col = lse_col - own_column(picked)
    loss_out[...] = jnp.sum(jnp.where(eye, loss_col, 0.0), axis=0, keepdims=True)
    for copy in (*t_copies[2:], *pp_copies[2:]):
        copy.wait_recv()

    def query_sum(n, carry):
        terms = tf[x, :, columns(n)]
        paired_rows = pps[x, :, columns(n)].astype(F32)
        for side in range(2):
            terms = terms + t_in[side, :, columns(n)].astype(F32)
            paired_rows = paired_rows + pp_in[side, :, columns(n)].astype(F32)
        hard = neg[:, columns(n)].astype(F32) - paired_rows
        qd_out[:, columns(n)] = (SCALE * (alpha_col * terms + hard_weight_col * hard)).astype(BF)
        return carry

    lax.fori_loop(0, chunks, query_sum, 0)

    each_partner(lambda t: weight(t).wait_recv())
    hw_in[pl.ds(pl.multiple_of(dp * 8, 8), 8), :] = hw[pl.ds(pl.multiple_of(dp * 8, 8), 8), :]
    hard_high, hard_low = split(by_asked(hw_in[every_8th, :]).T)

    def widen_q(t):
        push(t).wait_recv()
        widen(qscr, qrecv, Q_ROWS, dp_peer(t)[1])

    widen(qscr, qrecv, Q_ROWS, dp)
    each_partner(widen_q)
    gather_rows(qn, place_q)
    dp_here.wait_recv()
    dp_y.wait_recv()

    def passage_sum(n, carry):
        terms = qn[:, columns(n)]
        out = dpf[mine, :, columns(n)] + SCALE * (dot(hard_high, terms) + dot(hard_low, terms))
        out = out + dpc_in[0, :, columns(n)].astype(F32) + dpy_in[:, columns(n)].astype(F32)
        pg_out[:, columns(n)] = out.astype(BF)
        return carry

    lax.fori_loop(0, chunks, passage_sum, 0)

    for copy in (q_right, q_left, q_on, q_back, p_core, p_across, p_pass, *st_copies, *t_copies, *pp_copies, *al_copies):
        copy.wait_send()
    for copy in (dp_across, dp_here, dp_y):
        copy.wait_send()

    def sent(t):
        request(t).wait_send()
        fetch(t).wait_send()
        push(t).wait_send()
        weight(t).wait_send()

    each_partner(sent)


def shards(queries, passages, positive, hard_owner, hard_slot):
    q, p = queries[0], passages[0]
    rows, width = q.shape
    wide = N_X * rows
    vmem = pl.BlockSpec(memory_space=pltpu.VMEM)
    anywhere = pl.BlockSpec(memory_space=pl.ANY)
    block, halves = (rows, width), (rows, width // 2)
    loss, qd, pg = pl.pallas_call(
        kernel,
        out_shape=(pltpu.VMEM((1, rows), F32), pltpu.VMEM(block, BF), pltpu.VMEM(block, BF)),
        in_specs=[vmem] * 3 + [anywhere] * 2,
        out_specs=[vmem] * 3,
        scratch_shapes=[
            pltpu.VMEM((N_X, *block), BF),
            pltpu.VMEM((N_X, *block), BF),
            pltpu.VMEM((N_DP * P_ROWS, LANES), F32),
            pltpu.VMEM((N_DP * Q_ROWS, LANES), F32),
            pltpu.VMEM((N_DP, P_ROWS, LANES), BF),
            pltpu.VMEM((N_DP, Q_ROWS, LANES), BF),
            pltpu.VMEM((N_DP, P_ROWS, LANES), BF),
            pltpu.VMEM((N_DP, Q_ROWS, LANES), BF),
            pltpu.VMEM((N_DP * CAP, width), BF),
            pltpu.VMEM((N_DP * CAP, width), BF),
            pltpu.VMEM(block, BF),
            pltpu.VMEM((N_DP * 8, LANES), F32),
            pltpu.VMEM((N_DP * 8, LANES), F32),
            pltpu.VMEM((N_DP * 8, LANES), F32),
            pltpu.VMEM((N_DP * 8, LANES), F32),
            pltpu.VMEM((8, wide), F32),
            pltpu.VMEM((N_X, 8, wide), F32),
            pltpu.VMEM((8, wide), F32),
            pltpu.VMEM((N_X, 8, wide), F32),
            pltpu.VMEM((N_X, *block), F32),
            pltpu.VMEM((N_X, *block), BF),
            pltpu.VMEM((2, *block), BF),
            pltpu.VMEM((2, *halves), BF),
            pltpu.VMEM((2, *halves), BF),
            pltpu.VMEM((N_X, *block), BF),
            pltpu.VMEM((2, *block), BF),
            pltpu.VMEM((2, *halves), BF),
            pltpu.VMEM((2, *halves), BF),
            pltpu.VMEM((N_X, *block), F32),
            pltpu.VMEM((N_X, *block), BF),
            pltpu.VMEM((2, *block), BF),
            pltpu.VMEM(block, BF),
            pltpu.VMEM(block, BF),
            pltpu.SemaphoreType.DMA((N_SEM,)),
            pltpu.SemaphoreType.DMA((N_SEM,)),
            pltpu.SemaphoreType.DMA((2,)),
        ],
        compiler_params=pltpu.CompilerParams(
            collective_id=0, has_side_effects=True, vmem_limit_bytes=56 * 2**20
        ),
        cost_estimate=pl.CostEstimate(flops=3 * 10**9, bytes_accessed=2 * 10**6, transcendentals=2 * 10**5),
    )(positive, hard_owner.reshape(1, rows), hard_slot.reshape(1, rows), q, p)
    return loss, qd[None], pg[None]


def solution(mesh):
    placed = (
        P("dp", "blk", None),
        P("dp", "blk", None),
        P("dp", None),
        P("dp", "blk", None),
        P("dp", "blk", None),
    )
    return jax.shard_map(
        shards,
        mesh=mesh,
        in_specs=placed,
        out_specs=(P("dp", "blk"), P("dp", "blk", None), P("dp", "blk", None)),
        check_vma=False,
    )
```

```python
import functools

import jax
import jax.numpy as jnp
from jax import lax
from jax.experimental import pallas as pl
from jax.experimental.pallas import tpu as pltpu
from jax.sharding import PartitionSpec as P

SCALE = 50.0
MESH = pl.DeviceIdType.MESH
N_X, N_Z, N_DP, CAP = 4, 16, 32, 3
LANES = 128
P_ROWS, Q_ROWS = 96, 80
CHUNK = 512
BF, F32 = jnp.bfloat16, jnp.float32

S_Q, S_P, S_ST, S_DP, S_AL, S_DQ, S_PP, S_REQ, S_PF, S_QP, S_HW = 0, 4, 8, 12, 16, 20, 26, 32, 64, 96, 128
N_SEM = 160
EARLY = 4


def iota(shape, dim):
    return lax.broadcasted_iota(jnp.int32, shape, dim)


def dot(a, b, contract=((1,), (0,))):
    return lax.dot_general(a, b, (contract, ((), ())), preferred_element_type=F32)


def split(a):
    high = a.astype(BF)
    return high, (a - high.astype(F32)).astype(BF)


def kernel(
    positive, owner, slot, q_in, p_in, loss_out, qd_out, pg_out,
    qg, pc, pscr, qscr, pbuf, qbuf, precv, qrecv, pn, qn, neg,
    req, req_in, hw, hw_in, stats, stats_in, alphas, alphas_in,
    tf, ts, t_in, t_pass, t_sum, pps, pp_in, pp_pass, pp_sum, dpf, dps, dpc_in, dpy, dpy_in,
    send, recv, local,
):
    rows, width = q_in.shape
    wide = N_X * rows
    chunks = width // CHUNK
    blk, dp = lax.axis_index("blk"), lax.axis_index("dp")
    core, x, yh = lax.rem(blk, 2), lax.rem(blk // 2, N_X), blk // (2 * N_X)
    z, yl = lax.rem(dp, N_Z), dp // N_Z
    other_core, other_yh = blk + 1 - 2 * core, blk + 2 * N_X - 4 * N_X * yh
    mine, across = yh * 2 + core, (1 - yh) * 2 + core

    def x_peer(d):
        to = lax.rem(x + d, N_X)
        return to, (yh * N_X + to) * 2 + core

    right_x, right = x_peer(1)
    left_x, left = x_peer(N_X - 1)
    opposite = lax.rem(x + 2, N_X)
    half = width // 2
    low_half, high_half = pl.ds(0, half), pl.ds(half, half)

    def dp_peer(t):
        dy = lax.rem(t, 2)
        k = t // 2
        half = (k + 1) // 2
        odd = lax.rem(k, 2)
        dz = lax.rem(N_Z // 2 + half - 2 * half * odd + N_Z, N_Z)
        y = lax.rem(yl + dy, 2) * N_Z
        return y + lax.rem(z + dz, N_Z), y + lax.rem(z - dz + N_Z, N_Z)

    self_t = 2 * (N_Z - 1)

    def each_partner(act, first=0):
        def step(t, carry):
            act(t)
            return carry

        lax.fori_loop(first, self_t, step, 0)
        act(self_t + 1)

    def remote(src, dst, sem, **to):
        return pltpu.make_async_remote_copy(
            src_ref=src,
            dst_ref=dst,
            send_sem=send.at[sem],
            recv_sem=recv.at[sem],
            device_id={"blk": blk, "dp": dp, **to},
            device_id_type=MESH,
        )

    barrier = pltpu.get_barrier_semaphore()

    def greet(**to):
        pl.semaphore_signal(barrier, inc=1, device_id={"blk": blk, "dp": dp, **to}, device_id_type=MESH)

    each_partner(lambda t: greet(dp=dp_peer(t)[0]))
    for d in range(1, N_X):
        greet(blk=x_peer(d)[1])
    greet(blk=other_core)
    greet(blk=other_yh)

    keep_q = pltpu.make_async_copy(q_in, qg.at[x], local.at[0])
    keep_p = pltpu.make_async_copy(p_in, pc.at[mine], local.at[1])
    keep_q.start()
    keep_p.start()

    owner_row = owner[...].astype(F32)
    slot_row = slot[...].astype(F32)
    r0, r1 = iota((rows, rows), 0), iota((rows, rows), 1)
    eye = r0 == r1

    def column(row):
        return jnp.sum(jnp.where(eye, row, 0.0), axis=1, keepdims=True)

    owner_col = column(owner_row)
    same = jnp.where(owner_col == owner_row, 1.0, 0.0)
    rank_col = jnp.sum(jnp.where(r1 < r0, same, 0.0), axis=1, keepdims=True)
    rank_row = jnp.sum(jnp.where(r0 < r1, same, 0.0), axis=0, keepdims=True)
    key_row = rank_row * N_DP + owner_row
    key_col = rank_col * N_DP + owner_col
    slots = N_DP * CAP
    by_slot = key_row == iota((slots, rows), 0).astype(F32)
    by_row = key_col == iota((rows, slots), 1).astype(F32)
    lane = iota((N_DP, LANES), 1)

    def table(row):
        out = jnp.zeros((N_DP, LANES), F32)
        for c in range(CAP):
            picked = jnp.where(by_slot[c * N_DP : (c + 1) * N_DP], row, 0.0)
            out = jnp.where(lane == c, jnp.sum(picked, axis=1, keepdims=True), out)
        return out

    every_8th = pl.ds(0, N_DP, stride=8)
    req[...] = jnp.zeros_like(req)
    req[every_8th, :] = table(slot_row + 1.0)
    hw[...] = jnp.zeros_like(hw)
    stats[...] = jnp.zeros_like(stats)
    alphas[...] = jnp.zeros_like(alphas)
    pscr[...] = jnp.zeros_like(pscr)

    def columns(n):
        return pl.ds(pl.multiple_of(n * CHUNK, CHUNK), CHUNK)

    def lay_out(onehot, ref_of, place):
        for n in range(chunks):
            packed = dot(onehot, ref_of(n))
            for c in range(CAP):
                for k in range(CHUNK // LANES):
                    ref, at, stride = place(c * (width // LANES) + n * (CHUNK // LANES) + k)
                    ref[pl.ds(at, N_DP, stride=stride), :] = packed[
                        c * N_DP : (c + 1) * N_DP, k * LANES : (k + 1) * LANES
                    ]

    def place_q(i):
        return (qscr, i, Q_ROWS) if i < Q_ROWS else (pscr, 84 + i - Q_ROWS, P_ROWS)

    def place_p(i):
        return (pscr, i, P_ROWS)

    keep_q.wait()
    lay_out(
        jnp.where(by_slot, 1.0, 0.0).astype(BF),
        lambda n: qg[x, :, n * CHUNK : (n + 1) * CHUNK],
        place_q,
    )

    def round_q(a, carry):
        qbuf[a] = qscr[pl.ds(pl.multiple_of(a * Q_ROWS, 16), Q_ROWS), :].astype(BF)
        return carry

    lax.fori_loop(0, N_DP, round_q, 0)
    keep_p.wait()
    pl.semaphore_wait(barrier, N_X + 1 + N_DP - 1)

    def table_copy(src, dst, base, t):
        to, _ = dp_peer(t)
        return remote(
            src.at[pl.ds(pl.multiple_of(to * 8, 8), 8)],
            dst.at[pl.ds(pl.multiple_of(dp * 8, 8), 8)],
            base + t,
            dp=to,
        )

    def rows_copy(src, dst, base, t):
        to, _ = dp_peer(t)
        return remote(src.at[to], dst.at[dp], base + t, dp=to)

    request = functools.partial(table_copy, req, req_in, S_REQ)
    weight = functools.partial(table_copy, hw, hw_in, S_HW)
    fetch = functools.partial(rows_copy, pbuf, precv, S_PF)
    push = functools.partial(rows_copy, qbuf, qrecv, S_QP)

    each_partner(lambda t: request(t).start())
    for t in range(EARLY):
        push(t).start()

    q_right = remote(qg.at[x], qg.at[x], S_Q, blk=right)
    q_left = remote(qg.at[x], qg.at[x], S_Q + 1, blk=left)
    p_core = remote(pc.at[mine], pc.at[mine], S_P, blk=other_core)
    p_across = remote(pc.at[mine], pc.at[mine], S_P + 1, blk=other_yh)
    p_across.start()
    q_right.start()
    q_left.start()
    p_core.start()

    each_partner(lambda t: request(t).wait_recv())
    req_in[pl.ds(pl.multiple_of(dp * 8, 8), 8), :] = req[pl.ds(pl.multiple_of(dp * 8, 8), 8), :]
    asked = req_in[every_8th, :] - 1.0

    def by_asked(values):
        row_of = iota((N_DP, rows), 1).astype(F32)
        return jnp.concatenate(
            [jnp.where(asked[:, c : c + 1] == row_of, values[:, c : c + 1], 0.0) for c in range(CAP)],
            axis=0,
        )

    lay_out(
        by_asked(jnp.ones((N_DP, LANES), F32)).astype(BF),
        lambda n: pc[mine, :, n * CHUNK : (n + 1) * CHUNK],
        place_p,
    )

    def round_p(a, carry):
        pbuf[a] = pscr[pl.ds(pl.multiple_of(a * P_ROWS, 16), P_ROWS), :].astype(BF)
        return carry

    lax.fori_loop(0, N_DP, round_p, 0)
    each_partner(lambda t: fetch(t).start())
    each_partner(lambda t: push(t).start(), EARLY)
    precv[dp] = pbuf[dp]
    qrecv[dp] = qbuf[dp]

    p_across.wait_recv()
    p_pass = remote(pc.at[across], pc.at[across], S_P + 2, blk=other_core)
    p_pass.start()
    q_right.wait_recv()
    q_on = remote(qg.at[left_x, :, low_half], qg.at[left_x, :, low_half], S_Q + 2, blk=right)
    q_on.start()
    q_left.wait_recv()
    q_back = remote(qg.at[right_x, :, high_half], qg.at[right_x, :, high_half], S_Q + 3, blk=left)
    q_back.start()

    lanes = iota((8, LANES), 1)
    halves = []
    for i in range(N_X):
        chunk = positive[0:1, pl.ds(pl.multiple_of((yh * N_X + i) * LANES, LANES), LANES)]
        chunk = jnp.broadcast_to(chunk, (8, LANES))
        halves.append(jnp.where(core == i % 2, chunk, pltpu.roll(chunk, rows, 1)))
    positive_wide = jnp.concatenate(
        [jnp.where(lanes < rows, halves[i], halves[i + 1]) for i in range(0, N_X, 2)], axis=1
    )[0:1, :]
    row = iota((wide, 1), 0)
    index = ((row // (2 * rows)) * N_X + x) * 2 * rows + lax.rem(row, 2 * rows)
    paired = jnp.where(index == positive_wide, 1.0, 0.0)

    p_core.wait_recv()
    p_pass.wait_recv()

    pairs = paired.astype(BF)
    pairs_by_query = paired.T.astype(BF)

    def ring_first(blocks, passing, into, base):
        copies = [
            remote(blocks.at[opposite, :, low_half], passing.at[0], base, blk=right),
            remote(blocks.at[opposite, :, high_half], passing.at[1], base + 1, blk=left),
            remote(blocks.at[right_x, :, high_half], into.at[0, :, high_half], base + 2, blk=right),
            remote(blocks.at[left_x, :, low_half], into.at[1, :, low_half], base + 3, blk=left),
        ]
        for copy in copies:
            copy.start()
        return copies

    def ring_second(copies, blocks, passing, sums, into, base):
        copies[0].wait_recv()
        copies[1].wait_recv()
        size = half // chunks

        def add(n, carry):
            at = pl.ds(pl.multiple_of(n * size, size), size)
            beyond = pl.ds(pl.multiple_of(half + n * size, size), size)
            sums[0, :, at] = (blocks[right_x, :, at].astype(F32) + passing[0, :, at].astype(F32)).astype(BF)
            sums[1, :, at] = (blocks[left_x, :, beyond].astype(F32) + passing[1, :, at].astype(F32)).astype(BF)
            return carry

        lax.fori_loop(0, chunks, add, 0)
        more = [
            remote(sums.at[0], into.at[0, :, low_half], base + 4, blk=right),
            remote(sums.at[1], into.at[1, :, high_half], base + 5, blk=left),
        ]
        for copy in more:
            copy.start()
        return copies + more

    q_on.wait_recv()
    q_back.wait_recv()

    def add_scores(n, total):
        return total + dot(
            pc[:, :, columns(n)].reshape(wide, CHUNK),
            qg[:, :, columns(n)].reshape(wide, CHUNK),
            ((1,), (1,)),
        )

    scores = SCALE * lax.fori_loop(0, chunks, add_scores, jnp.zeros((wide, wide), F32))
    peak = jnp.max(scores, axis=0, keepdims=True)
    stats[0:1, :] = peak
    stats[1:2, :] = jnp.sum(jnp.exp(scores - peak), axis=0, keepdims=True)
    stats[2:3, :] = jnp.sum(paired * scores, axis=0, keepdims=True)
    st_copies = [remote(stats, stats_in.at[x], S_ST + d, blk=x_peer(d)[1]) for d in range(1, N_X)]
    for copy in st_copies:
        copy.start()
    stats_in[x] = stats[...]
    for copy in st_copies:
        copy.wait_recv()
    peaks = [stats_in[i, 0:1, :] for i in range(N_X)]
    top = functools.reduce(jnp.maximum, peaks)
    whole = sum(stats_in[i, 1:2, :] * jnp.exp(peaks[i] - top) for i in range(N_X))
    lse_batch = top + jnp.log(whole)
    picked = sum(stats_in[i, 2:3, :] for i in range(N_X))
    weights = jnp.exp(scores - lse_batch)
    high, low = split((weights - paired).T)

    def query_terms(n, carry):
        part = pc[:, :, columns(n)].reshape(wide, CHUNK)
        out = (dot(high, part) + dot(low, part)).reshape(N_X, rows, CHUNK)
        tf[:, :, columns(n)] = out
        ts[:, :, columns(n)] = out.astype(BF)
        return carry

    lax.fori_loop(0, chunks, query_terms, 0)
    t_copies = ring_first(ts, t_pass, t_in, S_DQ)
    def positives(n, carry):
        out = dot(pairs_by_query, pc[:, :, columns(n)].reshape(wide, CHUNK))
        pps[:, :, columns(n)] = out.reshape(N_X, rows, CHUNK).astype(BF)
        return carry

    lax.fori_loop(0, chunks, positives, 0)

    t_copies = ring_second(t_copies, tf, t_pass, t_sum, t_in, S_DQ)

    def widen_p(t):
        fetch(t).wait_recv()
        widen(pscr, precv, P_ROWS, dp_peer(t)[1])

    def widen(out, source, size, a):
        out[pl.ds(pl.multiple_of(a * size, 8), size), :] = source[a].astype(F32)

    widen(pscr, precv, P_ROWS, dp)
    each_partner(widen_p)

    def gather_rows(out, place):
        for n in range(width // LANES):
            for c in range(CAP):
                ref, at, stride = place(c * (width // LANES) + n)
                out[c * N_DP : (c + 1) * N_DP, n * LANES : (n + 1) * LANES] = ref[
                    pl.ds(at, N_DP, stride=stride), :
                ].astype(BF)

    gather_rows(pn, place_p)
    pick = jnp.where(by_row, 1.0, 0.0).astype(BF)

    def take_negatives(n, total):
        rows_of = dot(pick, pn[:, columns(n)])
        neg[:, columns(n)] = rows_of.astype(BF)
        return total + rows_of * qg[x, :, columns(n)].astype(F32)

    products = lax.fori_loop(0, chunks, take_negatives, jnp.zeros((rows, CHUNK), F32))
    hard_col = SCALE * jnp.sum(products, axis=1, keepdims=True)
    shifted = iota((rows, wide), 1) == iota((rows, wide), 0) + x * rows

    def own_column(wide_row):
        return jnp.sum(jnp.where(shifted, wide_row, 0.0), axis=1, keepdims=True)

    batch_col = own_column(lse_batch)
    top_col = jnp.maximum(batch_col, hard_col)
    lse_col = top_col + jnp.log(jnp.exp(batch_col - top_col) + jnp.exp(hard_col - top_col))
    alpha_col = jnp.exp(batch_col - lse_col)
    hard_weight_col = jnp.exp(hard_col - lse_col)
    alphas[0:1, :] = jnp.sum(jnp.where(shifted, alpha_col, 0.0), axis=0, keepdims=True)
    al_copies = [remote(alphas, alphas_in.at[x], S_AL + d, blk=x_peer(d)[1]) for d in range(1, N_X)]
    for copy in al_copies:
        copy.start()
    pp_copies = ring_first(pps, pp_pass, pp_in, S_PP)
    alphas_in[x] = alphas[...]
    hard_weight_row = jnp.sum(jnp.where(eye, hard_weight_col, 0.0), axis=0, keepdims=True)
    hw[every_8th, :] = table(hard_weight_row)
    each_partner(lambda t: weight(t).start())
    for copy in al_copies:
        copy.wait_recv()
    alpha = sum(alphas_in[i, 0:1, :] for i in range(N_X))
    probs = (weights * alpha).astype(BF)

    size = half // chunks

    def piece(n):
        return pl.ds(pl.multiple_of(n * size, size), size)

    def passage_terms(n, carry):
        part = qg[:, :, piece(n)].reshape(wide, size)
        out = (SCALE * (dot(probs, part) - dot(pairs, part))).reshape(N_X, rows, size)
        dpf[:, :, piece(n)] = out
        dps[:, :, piece(n)] = out.astype(BF)
        return carry

    def sum_across(n, carry):
        dpy[:, piece(n)] = (dpf[across, :, piece(n)] + dpc_in[1, :, piece(n)].astype(F32)).astype(BF)
        return carry

    dp_across, dp_y = [], []
    for h, part_of in enumerate((low_half, high_half)):
        lax.fori_loop(h * chunks, (h + 1) * chunks, passage_terms, 0)
        copy = remote(
            dps.at[(1 - yh) * 2 + 1 - core, :, part_of], dpc_in.at[1, :, part_of], S_DP + h, blk=other_core
        )
        copy.start()
        dp_across.append(copy)
    for h, part_of in enumerate((low_half, high_half)):
        dp_across[h].wait_recv()
        lax.fori_loop(h * chunks, (h + 1) * chunks, sum_across, 0)
        copy = remote(dpy.at[:, part_of], dpy_in.at[:, part_of], S_DP + 2 + h, blk=other_yh)
        copy.start()
        dp_y.append(copy)
    dp_here = remote(dps.at[yh * 2 + 1 - core], dpc_in.at[0], S_P + 3, blk=other_core)
    dp_here.start()
    pp_copies = ring_second(pp_copies, pps, pp_pass, pp_sum, pp_in, S_PP)

    loss_col = lse_col - own_column(picked)
    loss_out[...] = jnp.sum(jnp.where(eye, loss_col, 0.0), axis=0, keepdims=True)
    for copy in (*t_copies[2:], *pp_copies[2:]):
        copy.wait_recv()

    def query_sum(n, carry):
        terms = tf[x, :, columns(n)]
        paired_rows = pps[x, :, columns(n)].astype(F32)
        for side in range(2):
            terms = terms + t_in[side, :, columns(n)].astype(F32)
            paired_rows = paired_rows + pp_in[side, :, columns(n)].astype(F32)
        hard = neg[:, columns(n)].astype(F32) - paired_rows
        qd_out[:, columns(n)] = (SCALE * (alpha_col * terms + hard_weight_col * hard)).astype(BF)
        return carry

    lax.fori_loop(0, chunks, query_sum, 0)

    each_partner(lambda t: weight(t).wait_recv())
    hw_in[pl.ds(pl.multiple_of(dp * 8, 8), 8), :] = hw[pl.ds(pl.multiple_of(dp * 8, 8), 8), :]
    hard_high, hard_low = split(by_asked(hw_in[every_8th, :]).T)

    def widen_q(t):
        push(t).wait_recv()
        widen(qscr, qrecv, Q_ROWS, dp_peer(t)[1])

    widen(qscr, qrecv, Q_ROWS, dp)
    each_partner(widen_q)
    gather_rows(qn, place_q)
    dp_here.wait_recv()
    for copy in dp_y:
        copy.wait_recv()

    def passage_sum(n, carry):
        terms = qn[:, columns(n)]
        out = dpf[mine, :, columns(n)] + SCALE * (dot(hard_high, terms) + dot(hard_low, terms))
        out = out + dpc_in[0, :, columns(n)].astype(F32) + dpy_in[:, columns(n)].astype(F32)
        pg_out[:, columns(n)] = out.astype(BF)
        return carry

    lax.fori_loop(0, chunks, passage_sum, 0)

    for copy in (q_right, q_left, q_on, q_back, p_core, p_across, p_pass, *st_copies, *t_copies, *pp_copies, *al_copies):
        copy.wait_send()
    for copy in (*dp_across, dp_here, *dp_y):
        copy.wait_send()

    def sent(t):
        request(t).wait_send()
        fetch(t).wait_send()
        push(t).wait_send()
        weight(t).wait_send()

    each_partner(sent)


def shards(queries, passages, positive, hard_owner, hard_slot):
    q, p = queries[0], passages[0]
    rows, width = q.shape
    wide = N_X * rows
    vmem = pl.BlockSpec(memory_space=pltpu.VMEM)
    anywhere = pl.BlockSpec(memory_space=pl.ANY)
    block, halves = (rows, width), (rows, width // 2)
    loss, qd, pg = pl.pallas_call(
        kernel,
        out_shape=(pltpu.VMEM((1, rows), F32), pltpu.VMEM(block, BF), pltpu.VMEM(block, BF)),
        in_specs=[vmem] * 3 + [anywhere] * 2,
        out_specs=[vmem] * 3,
        scratch_shapes=[
            pltpu.VMEM((N_X, *block), BF),
            pltpu.VMEM((N_X, *block), BF),
            pltpu.VMEM((N_DP * P_ROWS, LANES), F32),
            pltpu.VMEM((N_DP * Q_ROWS, LANES), F32),
            pltpu.VMEM((N_DP, P_ROWS, LANES), BF),
            pltpu.VMEM((N_DP, Q_ROWS, LANES), BF),
            pltpu.VMEM((N_DP, P_ROWS, LANES), BF),
            pltpu.VMEM((N_DP, Q_ROWS, LANES), BF),
            pltpu.VMEM((N_DP * CAP, width), BF),
            pltpu.VMEM((N_DP * CAP, width), BF),
            pltpu.VMEM(block, BF),
            pltpu.VMEM((N_DP * 8, LANES), F32),
            pltpu.VMEM((N_DP * 8, LANES), F32),
            pltpu.VMEM((N_DP * 8, LANES), F32),
            pltpu.VMEM((N_DP * 8, LANES), F32),
            pltpu.VMEM((8, wide), F32),
            pltpu.VMEM((N_X, 8, wide), F32),
            pltpu.VMEM((8, wide), F32),
            pltpu.VMEM((N_X, 8, wide), F32),
            pltpu.VMEM((N_X, *block), F32),
            pltpu.VMEM((N_X, *block), BF),
            pltpu.VMEM((2, *block), BF),
            pltpu.VMEM((2, *halves), BF),
            pltpu.VMEM((2, *halves), BF),
            pltpu.VMEM((N_X, *block), BF),
            pltpu.VMEM((2, *block), BF),
            pltpu.VMEM((2, *halves), BF),
            pltpu.VMEM((2, *halves), BF),
            pltpu.VMEM((N_X, *block), F32),
            pltpu.VMEM((N_X, *block), BF),
            pltpu.VMEM((2, *block), BF),
            pltpu.VMEM(block, BF),
            pltpu.VMEM(block, BF),
            pltpu.SemaphoreType.DMA((N_SEM,)),
            pltpu.SemaphoreType.DMA((N_SEM,)),
            pltpu.SemaphoreType.DMA((2,)),
        ],
        compiler_params=pltpu.CompilerParams(
            collective_id=0, has_side_effects=True, vmem_limit_bytes=56 * 2**20
        ),
        cost_estimate=pl.CostEstimate(flops=3 * 10**9, bytes_accessed=2 * 10**6, transcendentals=2 * 10**5),
    )(positive, hard_owner.reshape(1, rows), hard_slot.reshape(1, rows), q, p)
    return loss, qd[None], pg[None]


def solution(mesh):
    placed = (
        P("dp", "blk", None),
        P("dp", "blk", None),
        P("dp", None),
        P("dp", "blk", None),
        P("dp", "blk", None),
    )
    return jax.shard_map(
        shards,
        mesh=mesh,
        in_specs=placed,
        out_specs=(P("dp", "blk"), P("dp", "blk", None), P("dp", "blk", None)),
        check_vma=False,
    )
```

```python
import functools

import jax
import jax.numpy as jnp
from jax import lax
from jax.experimental import pallas as pl
from jax.experimental.pallas import tpu as pltpu
from jax.sharding import PartitionSpec as P

SCALE = 50.0
MESH = pl.DeviceIdType.MESH
N_X, N_Z, N_DP, CAP = 4, 16, 32, 3
LANES = 128
P_ROWS, Q_ROWS = 96, 80
CHUNK = 512
BF, F32 = jnp.bfloat16, jnp.float32

S_Q, S_P, S_ST, S_DP, S_AL, S_DQ, S_PP, S_REQ, S_PF, S_QP, S_HW = 0, 4, 8, 12, 16, 20, 26, 32, 64, 96, 128
N_SEM = 160
EARLY = 4


def iota(shape, dim):
    return lax.broadcasted_iota(jnp.int32, shape, dim)


def dot(a, b, contract=((1,), (0,))):
    return lax.dot_general(a, b, (contract, ((), ())), preferred_element_type=F32)


def split(a):
    high = a.astype(BF)
    return high, (a - high.astype(F32)).astype(BF)


def kernel(
    positive, owner, slot, q_in, p_in, loss_out, qd_out, pg_out,
    qg, pc, pscr, qscr, pbuf, qbuf, precv, qrecv, pn, qn, neg,
    req, req_in, hw, hw_in, stats, stats_in, alphas, alphas_in,
    tf, ts, t_in, t_pass, t_sum, pps, pp_in, pp_pass, pp_sum, dpf, dps, dpc_in, dpy, dpy_in,
    send, recv, local,
):
    rows, width = q_in.shape
    wide = N_X * rows
    chunks = width // CHUNK
    blk, dp = lax.axis_index("blk"), lax.axis_index("dp")
    core, x, yh = lax.rem(blk, 2), lax.rem(blk // 2, N_X), blk // (2 * N_X)
    z, yl = lax.rem(dp, N_Z), dp // N_Z
    other_core, other_yh = blk + 1 - 2 * core, blk + 2 * N_X - 4 * N_X * yh
    mine, across = yh * 2 + core, (1 - yh) * 2 + core

    def x_peer(d):
        to = lax.rem(x + d, N_X)
        return to, (yh * N_X + to) * 2 + core

    right_x, right = x_peer(1)
    left_x, left = x_peer(N_X - 1)
    opposite = lax.rem(x + 2, N_X)
    half = width // 2
    low_half, high_half = pl.ds(0, half), pl.ds(half, half)

    def dp_peer(t):
        dy = lax.rem(t, 2)
        k = t // 2
        half = (k + 1) // 2
        odd = lax.rem(k, 2)
        dz = lax.rem(N_Z // 2 + half - 2 * half * odd + N_Z, N_Z)
        y = lax.rem(yl + dy, 2) * N_Z
        return y + lax.rem(z + dz, N_Z), y + lax.rem(z - dz + N_Z, N_Z)

    self_t = 2 * (N_Z - 1)

    def each_partner(act, first=0):
        def step(t, carry):
            act(t)
            return carry

        lax.fori_loop(first, self_t, step, 0)
        act(self_t + 1)

    def remote(src, dst, sem, **to):
        return pltpu.make_async_remote_copy(
            src_ref=src,
            dst_ref=dst,
            send_sem=send.at[sem],
            recv_sem=recv.at[sem],
            device_id={"blk": blk, "dp": dp, **to},
            device_id_type=MESH,
        )

    barrier = pltpu.get_barrier_semaphore()

    def greet(**to):
        pl.semaphore_signal(barrier, inc=1, device_id={"blk": blk, "dp": dp, **to}, device_id_type=MESH)

    each_partner(lambda t: greet(dp=dp_peer(t)[0]))
    for d in range(1, N_X):
        greet(blk=x_peer(d)[1])
    greet(blk=other_core)
    greet(blk=other_yh)

    keep_q = pltpu.make_async_copy(q_in, qg.at[x], local.at[0])
    keep_p = pltpu.make_async_copy(p_in, pc.at[mine], local.at[1])
    keep_q.start()
    keep_p.start()

    owner_row = owner[...].astype(F32)
    slot_row = slot[...].astype(F32)
    r0, r1 = iota((rows, rows), 0), iota((rows, rows), 1)
    eye = r0 == r1

    def column(row):
        return jnp.sum(jnp.where(eye, row, 0.0), axis=1, keepdims=True)

    owner_col = column(owner_row)
    same = jnp.where(owner_col == owner_row, 1.0, 0.0)
    rank_col = jnp.sum(jnp.where(r1 < r0, same, 0.0), axis=1, keepdims=True)
    rank_row = jnp.sum(jnp.where(r0 < r1, same, 0.0), axis=0, keepdims=True)
    key_row = rank_row * N_DP + owner_row
    key_col = rank_col * N_DP + owner_col
    slots = N_DP * CAP
    by_slot = key_row == iota((slots, rows), 0).astype(F32)
    by_row = key_col == iota((rows, slots), 1).astype(F32)
    lane = iota((N_DP, LANES), 1)

    def table(row):
        out = jnp.zeros((N_DP, LANES), F32)
        for c in range(CAP):
            picked = jnp.where(by_slot[c * N_DP : (c + 1) * N_DP], row, 0.0)
            out = jnp.where(lane == c, jnp.sum(picked, axis=1, keepdims=True), out)
        return out

    every_8th = pl.ds(0, N_DP, stride=8)
    req[...] = jnp.zeros_like(req)
    req[every_8th, :] = table(slot_row + 1.0)
    hw[...] = jnp.zeros_like(hw)
    stats[...] = jnp.zeros_like(stats)
    alphas[...] = jnp.zeros_like(alphas)
    pscr[...] = jnp.zeros_like(pscr)

    def columns(n):
        return pl.ds(pl.multiple_of(n * CHUNK, CHUNK), CHUNK)

    def lay_out(onehot, ref_of, place):
        for n in range(chunks):
            packed = dot(onehot, ref_of(n))
            for c in range(CAP):
                for k in range(CHUNK // LANES):
                    ref, at, stride = place(c * (width // LANES) + n * (CHUNK // LANES) + k)
                    ref[pl.ds(at, N_DP, stride=stride), :] = packed[
                        c * N_DP : (c + 1) * N_DP, k * LANES : (k + 1) * LANES
                    ]

    def place_q(i):
        return (qscr, i, Q_ROWS) if i < Q_ROWS else (pscr, 84 + i - Q_ROWS, P_ROWS)

    def place_p(i):
        return (pscr, i, P_ROWS)

    keep_q.wait()
    lay_out(
        jnp.where(by_slot, 1.0, 0.0).astype(BF),
        lambda n: qg[x, :, n * CHUNK : (n + 1) * CHUNK],
        place_q,
    )

    def round_q(a, carry):
        qbuf[a] = qscr[pl.ds(pl.multiple_of(a * Q_ROWS, 16), Q_ROWS), :].astype(BF)
        return carry

    lax.fori_loop(0, N_DP, round_q, 0)
    keep_p.wait()
    pl.semaphore_wait(barrier, N_X + 1 + N_DP - 1)

    def table_copy(src, dst, base, t):
        to, _ = dp_peer(t)
        return remote(
            src.at[pl.ds(pl.multiple_of(to * 8, 8), 8)],
            dst.at[pl.ds(pl.multiple_of(dp * 8, 8), 8)],
            base + t,
            dp=to,
        )

    def rows_copy(src, dst, base, t):
        to, _ = dp_peer(t)
        return remote(src.at[to], dst.at[dp], base + t, dp=to)

    request = functools.partial(table_copy, req, req_in, S_REQ)
    weight = functools.partial(table_copy, hw, hw_in, S_HW)
    fetch = functools.partial(rows_copy, pbuf, precv, S_PF)
    push = functools.partial(rows_copy, qbuf, qrecv, S_QP)

    each_partner(lambda t: request(t).start())
    for t in range(EARLY):
        push(t).start()

    q_right = remote(qg.at[x], qg.at[x], S_Q, blk=right)
    q_left = remote(qg.at[x], qg.at[x], S_Q + 1, blk=left)
    p_core = remote(pc.at[mine], pc.at[mine], S_P, blk=other_core)
    p_across = remote(pc.at[mine], pc.at[mine], S_P + 1, blk=other_yh)
    p_across.start()
    q_right.start()
    q_left.start()
    p_core.start()

    each_partner(lambda t: request(t).wait_recv())
    req_in[pl.ds(pl.multiple_of(dp * 8, 8), 8), :] = req[pl.ds(pl.multiple_of(dp * 8, 8), 8), :]
    asked = req_in[every_8th, :] - 1.0

    def by_asked(values):
        row_of = iota((N_DP, rows), 1).astype(F32)
        return jnp.concatenate(
            [jnp.where(asked[:, c : c + 1] == row_of, values[:, c : c + 1], 0.0) for c in range(CAP)],
            axis=0,
        )

    lay_out(
        by_asked(jnp.ones((N_DP, LANES), F32)).astype(BF),
        lambda n: pc[mine, :, n * CHUNK : (n + 1) * CHUNK],
        place_p,
    )

    def round_p(a, carry):
        pbuf[a] = pscr[pl.ds(pl.multiple_of(a * P_ROWS, 16), P_ROWS), :].astype(BF)
        return carry

    lax.fori_loop(0, N_DP, round_p, 0)
    each_partner(lambda t: fetch(t).start())
    each_partner(lambda t: push(t).start(), EARLY)
    precv[dp] = pbuf[dp]
    qrecv[dp] = qbuf[dp]

    p_across.wait_recv()
    p_pass = remote(pc.at[across], pc.at[across], S_P + 2, blk=other_core)
    p_pass.start()
    q_right.wait_recv()
    q_on = remote(qg.at[left_x, :, low_half], qg.at[left_x, :, low_half], S_Q + 2, blk=right)
    q_on.start()
    q_left.wait_recv()
    q_back = remote(qg.at[right_x, :, high_half], qg.at[right_x, :, high_half], S_Q + 3, blk=left)
    q_back.start()

    lanes = iota((8, LANES), 1)
    halves = []
    for i in range(N_X):
        chunk = positive[0:1, pl.ds(pl.multiple_of((yh * N_X + i) * LANES, LANES), LANES)]
        chunk = jnp.broadcast_to(chunk, (8, LANES))
        halves.append(jnp.where(core == i % 2, chunk, pltpu.roll(chunk, rows, 1)))
    positive_wide = jnp.concatenate(
        [jnp.where(lanes < rows, halves[i], halves[i + 1]) for i in range(0, N_X, 2)], axis=1
    )[0:1, :]
    row = iota((wide, 1), 0)
    index = ((row // (2 * rows)) * N_X + x) * 2 * rows + lax.rem(row, 2 * rows)
    paired = jnp.where(index == positive_wide, 1.0, 0.0)

    p_core.wait_recv()
    p_pass.wait_recv()

    pairs = paired.astype(BF)
    pairs_by_query = paired.T.astype(BF)

    def ring_first(blocks, passing, into, base):
        copies = [
            remote(blocks.at[opposite, :, low_half], passing.at[0], base, blk=right),
            remote(blocks.at[opposite, :, high_half], passing.at[1], base + 1, blk=left),
            remote(blocks.at[right_x, :, high_half], into.at[0, :, high_half], base + 2, blk=right),
            remote(blocks.at[left_x, :, low_half], into.at[1, :, low_half], base + 3, blk=left),
        ]
        for copy in copies:
            copy.start()
        return copies

    def ring_second(copies, blocks, passing, sums, into, base):
        copies[0].wait_recv()
        copies[1].wait_recv()
        size = half // chunks

        def add(n, carry):
            at = pl.ds(pl.multiple_of(n * size, size), size)
            beyond = pl.ds(pl.multiple_of(half + n * size, size), size)
            sums[0, :, at] = (blocks[right_x, :, at].astype(F32) + passing[0, :, at].astype(F32)).astype(BF)
            sums[1, :, at] = (blocks[left_x, :, beyond].astype(F32) + passing[1, :, at].astype(F32)).astype(BF)
            return carry

        lax.fori_loop(0, chunks, add, 0)
        more = [
            remote(sums.at[0], into.at[0, :, low_half], base + 4, blk=right),
            remote(sums.at[1], into.at[1, :, high_half], base + 5, blk=left),
        ]
        for copy in more:
            copy.start()
        return copies + more

    q_on.wait_recv()
    q_back.wait_recv()

    def add_scores(n, total):
        return total + dot(
            pc[:, :, columns(n)].reshape(wide, CHUNK),
            qg[:, :, columns(n)].reshape(wide, CHUNK),
            ((1,), (1,)),
        )

    scores = SCALE * lax.fori_loop(0, chunks, add_scores, jnp.zeros((wide, wide), F32))
    peak = jnp.max(scores, axis=0, keepdims=True)
    stats[0:1, :] = peak
    stats[1:2, :] = jnp.sum(jnp.exp(scores - peak), axis=0, keepdims=True)
    stats[2:3, :] = jnp.sum(paired * scores, axis=0, keepdims=True)
    st_copies = [remote(stats, stats_in.at[x], S_ST + d, blk=x_peer(d)[1]) for d in range(1, N_X)]
    for copy in st_copies:
        copy.start()
    stats_in[x] = stats[...]
    for copy in st_copies:
        copy.wait_recv()
    peaks = [stats_in[i, 0:1, :] for i in range(N_X)]
    top = functools.reduce(jnp.maximum, peaks)
    whole = sum(stats_in[i, 1:2, :] * jnp.exp(peaks[i] - top) for i in range(N_X))
    lse_batch = top + jnp.log(whole)
    picked = sum(stats_in[i, 2:3, :] for i in range(N_X))
    weights = jnp.exp(scores - lse_batch)
    high, low = split((weights - paired).T)

    def query_terms(n, carry):
        part = pc[:, :, columns(n)].reshape(wide, CHUNK)
        out = (dot(high, part) + dot(low, part)).reshape(N_X, rows, CHUNK)
        tf[:, :, columns(n)] = out
        ts[:, :, columns(n)] = out.astype(BF)
        return carry

    lax.fori_loop(0, chunks, query_terms, 0)
    t_copies = ring_first(ts, t_pass, t_in, S_DQ)
    def positives(n, carry):
        out = dot(pairs_by_query, pc[:, :, columns(n)].reshape(wide, CHUNK))
        pps[:, :, columns(n)] = out.reshape(N_X, rows, CHUNK).astype(BF)
        return carry

    lax.fori_loop(0, chunks, positives, 0)

    t_copies = ring_second(t_copies, tf, t_pass, t_sum, t_in, S_DQ)

    def widen_p(t):
        fetch(t).wait_recv()
        widen(pscr, precv, P_ROWS, dp_peer(t)[1])

    def widen(out, source, size, a):
        out[pl.ds(pl.multiple_of(a * size, 8), size), :] = source[a].astype(F32)

    widen(pscr, precv, P_ROWS, dp)
    each_partner(widen_p)

    def gather_rows(out, place):
        for n in range(width // LANES):
            for c in range(CAP):
                ref, at, stride = place(c * (width // LANES) + n)
                out[c * N_DP : (c + 1) * N_DP, n * LANES : (n + 1) * LANES] = ref[
                    pl.ds(at, N_DP, stride=stride), :
                ].astype(BF)

    gather_rows(pn, place_p)
    pick = jnp.where(by_row, 1.0, 0.0).astype(BF)

    def take_negatives(n, total):
        rows_of = dot(pick, pn[:, columns(n)])
        neg[:, columns(n)] = rows_of.astype(BF)
        return total + rows_of * qg[x, :, columns(n)].astype(F32)

    products = lax.fori_loop(0, chunks, take_negatives, jnp.zeros((rows, CHUNK), F32))
    hard_col = SCALE * jnp.sum(products, axis=1, keepdims=True)
    shifted = iota((rows, wide), 1) == iota((rows, wide), 0) + x * rows

    def own_column(wide_row):
        return jnp.sum(jnp.where(shifted, wide_row, 0.0), axis=1, keepdims=True)

    batch_col = own_column(lse_batch)
    top_col = jnp.maximum(batch_col, hard_col)
    lse_col = top_col + jnp.log(jnp.exp(batch_col - top_col) + jnp.exp(hard_col - top_col))
    alpha_col = jnp.exp(batch_col - lse_col)
    hard_weight_col = jnp.exp(hard_col - lse_col)
    alphas[0:1, :] = jnp.sum(jnp.where(shifted, alpha_col, 0.0), axis=0, keepdims=True)
    al_copies = [remote(alphas, alphas_in.at[x], S_AL + d, blk=x_peer(d)[1]) for d in range(1, N_X)]
    for copy in al_copies:
        copy.start()
    pp_copies = ring_first(pps, pp_pass, pp_in, S_PP)
    alphas_in[x] = alphas[...]
    hard_weight_row = jnp.sum(jnp.where(eye, hard_weight_col, 0.0), axis=0, keepdims=True)
    hw[every_8th, :] = table(hard_weight_row)
    each_partner(lambda t: weight(t).start())
    for copy in al_copies:
        copy.wait_recv()
    alpha = sum(alphas_in[i, 0:1, :] for i in range(N_X))
    probs = (weights * alpha).astype(BF)

    size = half // chunks

    def piece(n):
        return pl.ds(pl.multiple_of(n * size, size), size)

    def passage_terms(n, carry):
        part = qg[:, :, piece(n)].reshape(wide, size)
        out = (SCALE * (dot(probs, part) - dot(pairs, part))).reshape(N_X, rows, size)
        dpf[:, :, piece(n)] = out
        dps[:, :, piece(n)] = out.astype(BF)
        return carry

    def sum_across(n, carry):
        dpy[:, piece(n)] = (dpf[across, :, piece(n)] + dpc_in[1, :, piece(n)].astype(F32)).astype(BF)
        return carry

    dp_across, dp_y = [], []
    for h, part_of in enumerate((low_half, high_half)):
        lax.fori_loop(h * chunks, (h + 1) * chunks, passage_terms, 0)
        copy = remote(
            dps.at[(1 - yh) * 2 + 1 - core, :, part_of], dpc_in.at[1, :, part_of], S_DP + h, blk=other_core
        )
        copy.start()
        dp_across.append(copy)
    for h, part_of in enumerate((low_half, high_half)):
        dp_across[h].wait_recv()
        lax.fori_loop(h * chunks, (h + 1) * chunks, sum_across, 0)
        copy = remote(dpy.at[:, part_of], dpy_in.at[:, part_of], S_DP + 2 + h, blk=other_yh)
        copy.start()
        dp_y.append(copy)
    dp_here = remote(dps.at[yh * 2 + 1 - core], dpc_in.at[0], S_P + 3, blk=other_core)
    dp_here.start()
    pp_copies = ring_second(pp_copies, pps, pp_pass, pp_sum, pp_in, S_PP)

    loss_col = lse_col - own_column(picked)
    loss_out[...] = jnp.sum(jnp.where(eye, loss_col, 0.0), axis=0, keepdims=True)
    for copy in (*t_copies[2:], *pp_copies[2:]):
        copy.wait_recv()

    def query_sum(n, carry):
        terms = tf[x, :, columns(n)]
        paired_rows = pps[x, :, columns(n)].astype(F32)
        for side in range(2):
            terms = terms + t_in[side, :, columns(n)].astype(F32)
            paired_rows = paired_rows + pp_in[side, :, columns(n)].astype(F32)
        hard = neg[:, columns(n)].astype(F32) - paired_rows
        qd_out[:, columns(n)] = (SCALE * (alpha_col * terms + hard_weight_col * hard)).astype(BF)
        return carry

    lax.fori_loop(0, chunks, query_sum, 0)

    each_partner(lambda t: weight(t).wait_recv())
    hw_in[pl.ds(pl.multiple_of(dp * 8, 8), 8), :] = hw[pl.ds(pl.multiple_of(dp * 8, 8), 8), :]
    hard_high, hard_low = split(by_asked(hw_in[every_8th, :]).T)

    def sent_before(t):
        request(t).wait_send()
        fetch(t).wait_send()

    each_partner(sent_before)

    def widen_q(t):
        push(t).wait_recv()
        widen(qscr, qrecv, Q_ROWS, dp_peer(t)[1])

    widen(qscr, qrecv, Q_ROWS, dp)
    each_partner(widen_q)
    gather_rows(qn, place_q)
    dp_here.wait_recv()
    for copy in dp_y:
        copy.wait_recv()

    def passage_sum(n, carry):
        terms = qn[:, columns(n)]
        out = dpf[mine, :, columns(n)] + SCALE * (dot(hard_high, terms) + dot(hard_low, terms))
        out = out + dpc_in[0, :, columns(n)].astype(F32) + dpy_in[:, columns(n)].astype(F32)
        pg_out[:, columns(n)] = out.astype(BF)
        return carry

    lax.fori_loop(0, chunks, passage_sum, 0)

    for copy in (q_right, q_left, q_on, q_back, p_core, p_across, p_pass, *st_copies, *t_copies, *pp_copies, *al_copies):
        copy.wait_send()
    for copy in (*dp_across, dp_here, *dp_y):
        copy.wait_send()

    def sent(t):
        push(t).wait_send()
        weight(t).wait_send()

    each_partner(sent)


def shards(queries, passages, positive, hard_owner, hard_slot):
    q, p = queries[0], passages[0]
    rows, width = q.shape
    wide = N_X * rows
    vmem = pl.BlockSpec(memory_space=pltpu.VMEM)
    anywhere = pl.BlockSpec(memory_space=pl.ANY)
    block, halves = (rows, width), (rows, width // 2)
    loss, qd, pg = pl.pallas_call(
        kernel,
        out_shape=(pltpu.VMEM((1, rows), F32), pltpu.VMEM(block, BF), pltpu.VMEM(block, BF)),
        in_specs=[vmem] * 3 + [anywhere] * 2,
        out_specs=[vmem] * 3,
        scratch_shapes=[
            pltpu.VMEM((N_X, *block), BF),
            pltpu.VMEM((N_X, *block), BF),
            pltpu.VMEM((N_DP * P_ROWS, LANES), F32),
            pltpu.VMEM((N_DP * Q_ROWS, LANES), F32),
            pltpu.VMEM((N_DP, P_ROWS, LANES), BF),
            pltpu.VMEM((N_DP, Q_ROWS, LANES), BF),
            pltpu.VMEM((N_DP, P_ROWS, LANES), BF),
            pltpu.VMEM((N_DP, Q_ROWS, LANES), BF),
            pltpu.VMEM((N_DP * CAP, width), BF),
            pltpu.VMEM((N_DP * CAP, width), BF),
            pltpu.VMEM(block, BF),
            pltpu.VMEM((N_DP * 8, LANES), F32),
            pltpu.VMEM((N_DP * 8, LANES), F32),
            pltpu.VMEM((N_DP * 8, LANES), F32),
            pltpu.VMEM((N_DP * 8, LANES), F32),
            pltpu.VMEM((8, wide), F32),
            pltpu.VMEM((N_X, 8, wide), F32),
            pltpu.VMEM((8, wide), F32),
            pltpu.VMEM((N_X, 8, wide), F32),
            pltpu.VMEM((N_X, *block), F32),
            pltpu.VMEM((N_X, *block), BF),
            pltpu.VMEM((2, *block), BF),
            pltpu.VMEM((2, *halves), BF),
            pltpu.VMEM((2, *halves), BF),
            pltpu.VMEM((N_X, *block), BF),
            pltpu.VMEM((2, *block), BF),
            pltpu.VMEM((2, *halves), BF),
            pltpu.VMEM((2, *halves), BF),
            pltpu.VMEM((N_X, *block), F32),
            pltpu.VMEM((N_X, *block), BF),
            pltpu.VMEM((2, *block), BF),
            pltpu.VMEM(block, BF),
            pltpu.VMEM(block, BF),
            pltpu.SemaphoreType.DMA((N_SEM,)),
            pltpu.SemaphoreType.DMA((N_SEM,)),
            pltpu.SemaphoreType.DMA((2,)),
        ],
        compiler_params=pltpu.CompilerParams(
            collective_id=0, has_side_effects=True, vmem_limit_bytes=56 * 2**20
        ),
        cost_estimate=pl.CostEstimate(flops=3 * 10**9, bytes_accessed=2 * 10**6, transcendentals=2 * 10**5),
    )(positive, hard_owner.reshape(1, rows), hard_slot.reshape(1, rows), q, p)
    return loss, qd[None], pg[None]


def solution(mesh):
    placed = (
        P("dp", "blk", None),
        P("dp", "blk", None),
        P("dp", None),
        P("dp", "blk", None),
        P("dp", "blk", None),
    )
    return jax.shard_map(
        shards,
        mesh=mesh,
        in_specs=placed,
        out_specs=(P("dp", "blk"), P("dp", "blk", None), P("dp", "blk", None)),
        check_vma=False,
    )
```
